256 devices in a mesh: pair: 32 (over z_lo, x, core), virt: 8 (over y, z_hi).
Axes of the slice: x: 4, y: 4, z: 8 (z_hi: 2, z_lo: 4; z = z_hi * 4 + z_lo), core: 2. Of those that a mesh axis runs over, the one named last changes fastest.
Arguments:
- amplitudes: bfloat16 [96, 96, 128, 128], P('pair', None, 'virt'), may hold values from -6 to 6
- integrals: bfloat16 [128, 20, 128, 128], P('virt'), may hold values from -0.125 to 0.125
- cd_tiles: int32 [128, 20], P('virt'), may hold values from 0 to 127, as said below
- tile_counts: int32 [128], P('virt'), may hold values from 10 to 20, as said below
- eps_occ: float32 [96], replicated, may hold values from -2 to -0.5
- eps_virt: float32 [128], replicated, may hold values from 0.5 to 3
Outputs:
- new_amplitudes: bfloat16 [96, 96, 128, 128], P('pair', None, 'virt')
The draws below stay inside these ranges and needn't reach their ends.
Inputs may be any that keep to these rules, and one draw needn't show every extreme that they name: `cd_tiles`: row a holds 20 different numbers from lo(a) to lo(a) + 2 * 16 - 1, where lo(a) = min(max(a - 16, 0), 96); only its first tile_counts[a] entries are live. `tile_counts`: some entry equals 20.
All inputs are finite; a program needn't handle non-finite values.
Results may differ from the reference program's by a relative error of at most 0.001.
Values may be sent and summed in bfloat16 or wider, within the bound.
No kernel may reach another device: no remote copies, remote signals or barrier semaphores. Data moves between devices by JAX's collectives and lax.ppermute only.
A program may use at most 128 MiB of HBM per device.

```python
import jax
import jax.numpy as jnp
from jax import lax

O = 96
NVW = 128
CAP = 20
A_DEV = 16


def tile_table(key):
    base = jax.random.fold_in(key, 1234)
    first, second, third = jax.random.split(base, 3)
    counts = jax.random.randint(first, (NVW,), CAP - CAP // 2, CAP + 1)
    position = jax.random.randint(second, (), 0, NVW)
    positions = jnp.arange(NVW, dtype=jnp.int32)
    counts = jnp.where(positions == position, CAP, counts).astype(jnp.int32)
    lowest = jnp.clip(positions - A_DEV, 0, NVW - 2 * A_DEV)
    row_keys = jax.random.split(third, NVW)

    def permute_row(row_key):
        return jax.random.permutation(row_key, 2 * A_DEV)
    orders = jax.vmap(permute_row)(row_keys)
    tile_list = lowest[:, None] + orders[:, :CAP]
    return (tile_list.astype(jnp.int32), counts)


def draw_cd_tiles(key, part):
    return tile_table(key)[0]


def draw_tile_counts(key, part):
    return tile_table(key)[1]


def block_levels(stream_key, shape, cuts, low, high):
    factor_of, own = 1.0, jax.random.fold_in(stream_key, 6)
    for dim, blocks in cuts:
        steps = jnp.exp(jax.random.uniform(jax.random.fold_in(own, dim), (blocks,), jnp.float32, low / len(cuts), high / len(cuts)))
        factor_of = factor_of * jnp.repeat(steps, shape[dim] // blocks).reshape([-1 if axis == dim else 1 for axis in range(len(shape))])
    return factor_of


def scatter_about(key, dims, deviation, reach, shards=(), kind=jnp.bfloat16):
    drawn = jax.random.normal(key, dims, jnp.float32) * deviation
    if len(shards) > 0:
        drawn = block_levels(key, dims, shards, -0.22, 0.18) * drawn
    return jnp.clip(drawn, min=-reach, max=reach).astype(kind)


def setup_inputs(seed: int = 0) -> dict:
    streams_of = jax.random.split(jax.random.key(seed), 7)
    return {
        "amplitudes": scatter_about(streams_of[0], (O, O, NVW, NVW), 1.0, 6.0, ((0, 32), (2, 8))),
        "integrals": scatter_about(streams_of[1], (NVW, CAP, NVW, NVW), (CAP * NVW) ** -0.5, 0.125, ((0, 8),)),
        "cd_tiles": draw_cd_tiles(jax.random.fold_in(streams_of[6], 71), 0),
        "tile_counts": draw_tile_counts(jax.random.fold_in(streams_of[6], 71), 0),
        "eps_occ": jnp.clip(jax.random.uniform(streams_of[4], (O,), jnp.float32, -2.0, -0.5), -2.0, -0.5),
        "eps_virt": jnp.clip(jax.random.uniform(streams_of[5], (NVW,), jnp.float32, 0.5, 3.0), 0.5, 3.0),
    }


def reference(amplitudes, integrals, cd_tiles, tile_counts, eps_occ, eps_virt):
    slot_ids = jnp.arange(CAP, dtype=jnp.int32)
    live_slots = (slot_ids[None, :] < tile_counts[:, None]).astype(jnp.float32)

    def one_column(operands):
        tile_list, weights, kept = operands
        picked = jnp.take(amplitudes, tile_list.astype(jnp.int32), axis=2).astype(jnp.float32)
        masked = weights.astype(jnp.float32) * kept[:, None, None]
        return jnp.einsum("ijsd,sdb->ijb", picked, masked)

    ladder = lax.map(one_column, (cd_tiles, integrals, live_slots))
    ladder = jnp.transpose(ladder, (1, 2, 0, 3))
    symmetric = ladder + jnp.transpose(ladder, (1, 0, 3, 2))
    denominator = (eps_occ[:, None, None, None] + eps_occ[None, :, None, None]
                   - eps_virt[None, None, :, None] - eps_virt[None, None, None, :])
    return (symmetric / denominator).astype(jnp.bfloat16)
```

```python
import jax
import jax.numpy as jnp
from jax import lax
from jax.experimental import pallas as pl
from jax.experimental.pallas import tpu as pltpu
from jax.sharding import PartitionSpec as P

ROWS = 3
TILES = 16
VIRT = 8
LANES = 128
MSG = ROWS * ROWS * TILES * TILES // LANES


def exchange_groups(parts):
    parts = list(parts)
    group = lax.broadcasted_iota(jnp.int32, parts[0].shape, 1) // TILES
    for step in (1, 2, 4):
        upper = (group & step) != 0
        for p in range(8):
            if p & step:
                continue
            low, high = parts[p], parts[p + step]
            parts[p] = jnp.where(upper, pltpu.roll(high, TILES * step, 1), low)
            parts[p + step] = jnp.where(upper, high, pltpu.roll(low, LANES - TILES * step, 1))
    return parts


def ladder_kernel(index_ref, own_ref, over_ref, next_ref, weight_ref, out_ref, held, picked):
    step = pl.program_id(0)
    per_step = weight_ref.shape[0]
    slots = weight_ref.shape[1] // LANES

    @pl.when(step == 0)
    def _():
        held[0:TILES] = own_ref[...]
        held[TILES : 2 * TILES] = over_ref[...]
        held[2 * TILES : 3 * TILES] = next_ref[...]
        held[3 * TILES] = jnp.zeros_like(held[3 * TILES])

    for n in range(per_step):
        a = step * per_step + n
        for s in range(slots):
            picked[n, :, s * LANES : (s + 1) * LANES] = held[index_ref[a, s]]
        row = jnp.dot(picked[n], weight_ref[n], preferred_element_type=jnp.float32)
        out_ref[pl.ds(a, row.shape[0], stride=TILES), :] = row


def ladder_rows(index, own, over, beyond, weights):
    tiles, pairs, depth = own.shape
    k = weights.shape[1]
    per_step = 2
    whole = pl.BlockSpec((tiles, pairs, depth), lambda g, *_: (0, 0, 0))
    return pl.pallas_call(
        ladder_kernel,
        out_shape=jax.ShapeDtypeStruct((pairs * tiles, LANES), jnp.float32),
        grid_spec=pltpu.PrefetchScalarGridSpec(
            num_scalar_prefetch=1,
            grid=(tiles // per_step,),
            in_specs=[whole, whole, whole, pl.BlockSpec((per_step, k, LANES), lambda g, *_: (g, 0, 0))],
            out_specs=pl.BlockSpec((pairs * tiles, LANES), lambda g, *_: (0, 0)),
            scratch_shapes=[
                pltpu.VMEM((3 * tiles + 1, pairs, depth), jnp.bfloat16),
                pltpu.VMEM((per_step, pairs, k), jnp.bfloat16),
            ],
        ),
        compiler_params=pltpu.CompilerParams(vmem_limit_bytes=24 * 2**20),
        cost_estimate=pl.CostEstimate(
            flops=2 * pairs * k * LANES * tiles, bytes_accessed=2 * tiles * k * LANES, transcendentals=0
        ),
        name="ladder_rows",
    )(index, own, over, beyond, weights)


def pack_kernel(scale_ref, l0, l1, l2, out_ref, rest):
    ladders = (l0, l1, l2)
    scale = scale_ref[0]
    devices = out_ref.shape[0] // (VIRT * MSG)
    tile = ROWS * TILES

    @pl.loop(0, devices // 8)
    def _(octet):
        for half in range(2):
            parts = [
                l2[pl.ds(octet * 8 * tile + 2 * TILES + half * 8 + n, 8, stride=tile), :] for n in range(8)
            ]
            for v, part in enumerate(exchange_groups(parts)):
                rest[pl.ds(octet * 8 * TILES + 2 * v + half, 8, stride=TILES), :] = part

    @pl.loop(0, devices)
    def _(device):
        first = pl.multiple_of(device * tile, TILES)
        parts = [ladders[k // ROWS][pl.ds(first + (k % ROWS) * TILES, TILES), :] for k in range(8)]
        last = rest[pl.ds(pl.multiple_of(device * TILES, TILES), TILES), :]
        pieces = []
        for v, part in enumerate(exchange_groups(parts)):
            pieces += [part, last[2 * v : 2 * v + 2]]
        block = jnp.concatenate(pieces, axis=0) * scale
        out_ref[pl.ds(pl.multiple_of(device * VIRT * MSG, TILES), VIRT * MSG), :] = block.astype(out_ref.dtype)


def pack(scale, ladders):
    rows = ladders[0].shape[0] * len(ladders)
    return pl.pallas_call(
        pack_kernel,
        out_shape=jax.ShapeDtypeStruct((rows, LANES), jnp.float32),
        in_specs=[pl.BlockSpec(memory_space=pltpu.SMEM)] + [pl.BlockSpec(memory_space=pltpu.VMEM)] * 3,
        out_specs=pl.BlockSpec(memory_space=pltpu.VMEM),
        scratch_shapes=[pltpu.VMEM((rows // (ROWS * ROWS), LANES), jnp.float32)],
        compiler_params=pltpu.CompilerParams(vmem_limit_bytes=24 * 2**20),
        name="pack",
    )(scale, *ladders)


def finish_kernel(unscale_ref, occ_ref, own_occ_ref, got_ref, l0, l1, l2, va_ref, vb_ref, out_ref, rest, turned):
    ladders = (l0, l1, l2)
    unscale = unscale_ref[0]
    devices = got_ref.shape[0] // (VIRT * MSG)

    def store(i, j, partner):
        own = ladders[i][pl.ds(pl.multiple_of(j * TILES, TILES), TILES), :]
        bottom = (own_occ_ref[i] + occ_ref[j]) - va_ref[...] - vb_ref[...]
        out_ref[i, j] = ((own + partner) / bottom).astype(out_ref.dtype)

    @pl.loop(0, devices)
    def _(device):
        block = got_ref[pl.ds(pl.multiple_of(device * VIRT * MSG, TILES), VIRT * MSG), :].astype(jnp.float32)
        block = block * unscale
        cut = [block[v * MSG : (v + 1) * MSG] for v in range(VIRT)]
        main = jnp.concatenate([c[:TILES] for c in cut], axis=0).T
        rest[pl.ds(pl.multiple_of(device * TILES, TILES), TILES), :] = jnp.concatenate(
            [c[TILES:] for c in cut], axis=0
        )
        for k in range(8):
            store(k % ROWS, device * ROWS + k // ROWS, main[k * TILES : (k + 1) * TILES])

    @pl.loop(0, devices // 8)
    def _(octet):
        for half in range(2):
            parts = [rest[pl.ds(octet * 8 * TILES + 2 * v + half, 8, stride=TILES), :] for v in range(VIRT)]
            for n, part in enumerate(exchange_groups(parts)):
                turned[pl.ds(half * 8 + n, 8, stride=TILES), :] = part
        columns = turned[...].T
        parts = [columns[v * TILES : (v + 1) * TILES] for v in range(VIRT)]
        for n, part in enumerate(exchange_groups(parts)):
            store(ROWS - 1, (octet * 8 + n) * ROWS + ROWS - 1, part)


def finish(unscale, occ, own_occ, got, ladders, va, vb):
    partners = occ.shape[0]
    smem, vmem = pl.BlockSpec(memory_space=pltpu.SMEM), pl.BlockSpec(memory_space=pltpu.VMEM)
    return pl.pallas_call(
        finish_kernel,
        out_shape=jax.ShapeDtypeStruct((ROWS, partners, TILES, LANES), jnp.bfloat16),
        in_specs=[smem] * 3 + [vmem] * 6,
        out_specs=vmem,
        scratch_shapes=[
            pltpu.VMEM((got.shape[0] // (ROWS * ROWS), LANES), jnp.float32),
            pltpu.VMEM((LANES, LANES), jnp.float32),
        ],
        compiler_params=pltpu.CompilerParams(vmem_limit_bytes=24 * 2**20),
        name="finish",
    )(unscale, occ, own_occ, got, *ladders, va, vb)


def per_device(amplitudes, integrals, cd_tiles, tile_counts, eps_occ, eps_virt):
    rows, partners, tiles, depth = amplitudes.shape
    slots = integrals.shape[1]
    me = lax.axis_index("virt")
    swap = [(v, v ^ 1) for v in range(VIRT)]
    relay = [(v, v + 2) for v in range(0, VIRT - 2, 2)] + [(v, v - 2) for v in range(3, VIRT, 2)]
    own = [jnp.transpose(amplitudes[i], (1, 0, 2)) for i in range(rows)]
    over = [lax.ppermute(x, "virt", swap) for x in own]
    beyond = [lax.ppermute(x, "virt", relay) for x in over]

    live = lax.broadcasted_iota(jnp.int32, cd_tiles.shape, 1) < tile_counts[:, None]
    block = cd_tiles // tiles - me
    over_block = jnp.where(me % 2 == 0, 1, -1)
    place = jnp.where(block == 0, 0, jnp.where(block == over_block, 1, 2))
    index = jnp.where(live, place * tiles + cd_tiles % tiles, 3 * tiles).astype(jnp.int32)

    largest = jnp.stack(
        [
            jnp.max(jnp.abs(amplitudes)).astype(jnp.float32),
            jnp.max(jnp.where(live, jnp.max(jnp.abs(integrals), axis=(2, 3)), 0)).astype(jnp.float32),
        ]
    )
    largest = lax.pmax(largest, ("pair", "virt"))
    bound = jnp.maximum(largest[0] * largest[1] * (slots * depth), 1e-30)
    scale = (32768.0 / bound).reshape(1)
    unscale = (bound / 32768.0).reshape(1)

    weights = integrals.reshape(tiles, slots * depth, LANES)
    ladders = [ladder_rows(index, own[i], over[i], beyond[i], weights) for i in range(rows)]
    sent = pack(scale, ladders).astype(jnp.float16).reshape(-1, MSG // 2, 2, LANES)
    got = lax.all_to_all(sent, ("pair", "virt"), split_axis=0, concat_axis=0, tiled=True)
    own_occ = lax.dynamic_slice_in_dim(eps_occ, lax.axis_index("pair") * rows, rows)
    own_virt = lax.dynamic_slice_in_dim(eps_virt, me * tiles, tiles)
    return finish(
        unscale, eps_occ, own_occ, got.reshape(-1, LANES).astype(jnp.float32), ladders, own_virt[:, None], eps_virt[None, :]
    )


def solution(mesh):
    in_specs = (
        P("pair", None, "virt", None),
        P("virt", None, None, None),
        P("virt", None),
        P("virt"),
        P(),
        P(),
    )
    out_specs = P("pair", None, "virt", None)
    return jax.shard_map(
        per_device, mesh=mesh, in_specs=in_specs, out_specs=out_specs, check_vma=False
    )
```

```python
import jax
import jax.numpy as jnp
from jax import lax
from jax.experimental import pallas as pl
from jax.experimental.pallas import tpu as pltpu
from jax.sharding import PartitionSpec as P

ROWS = 3
TILES = 16
VIRT = 8
LANES = 128
VALUES = ROWS * ROWS * TILES * TILES // LANES
MSG = VALUES + 2


def exchange_groups(parts):
    parts = list(parts)
    group = lax.broadcasted_iota(jnp.int32, parts[0].shape, 1) // TILES
    for step in (1, 2, 4):
        upper = (group & step) != 0
        for p in range(8):
            if p & step:
                continue
            low, high = parts[p], parts[p + step]
            parts[p] = jnp.where(upper, pltpu.roll(high, TILES * step, 1), low)
            parts[p + step] = jnp.where(upper, high, pltpu.roll(low, LANES - TILES * step, 1))
    return parts


def ladder_kernel(index_ref, own_ref, over_ref, next_ref, weight_ref, out_ref, held, picked, weights, arrived):
    group = weights.shape[1]
    slots = weight_ref.shape[1] // LANES

    def fetch(step):
        return pltpu.make_async_copy(
            weight_ref.at[pl.ds(step * group, group)], weights.at[step % 2], arrived.at[step % 2]
        )

    fetch(0).start()
    held[0:TILES] = own_ref[...]
    held[TILES : 2 * TILES] = over_ref[...]
    held[2 * TILES : 3 * TILES] = next_ref[...]
    held[3 * TILES] = jnp.zeros_like(held[3 * TILES])
    for step in range(TILES // group):
        if step + 1 < TILES // group:
            fetch(step + 1).start()
        fetch(step).wait()
        for n in range(group):
            a = step * group + n
            for s in range(slots):
                picked[n, :, s * LANES : (s + 1) * LANES] = held[index_ref[a, s]]
            row = jnp.dot(picked[n], weights[step % 2, n], preferred_element_type=jnp.float32)
            out_ref[pl.ds(a, row.shape[0], stride=TILES), :] = row


def ladder_rows(index, own, over, beyond, weights):
    tiles, pairs, depth = own.shape
    k = weights.shape[1]
    group = 4
    smem, vmem = pl.BlockSpec(memory_space=pltpu.SMEM), pl.BlockSpec(memory_space=pltpu.VMEM)
    return pl.pallas_call(
        ladder_kernel,
        out_shape=jax.ShapeDtypeStruct((pairs * tiles, LANES), jnp.float32),
        in_specs=[smem] + [vmem] * 3 + [pl.BlockSpec(memory_space=pltpu.HBM)],
        out_specs=vmem,
        scratch_shapes=[
            pltpu.VMEM((3 * tiles + 1, pairs, depth), jnp.bfloat16),
            pltpu.VMEM((group, pairs, k), jnp.bfloat16),
            pltpu.VMEM((2, group, k, LANES), jnp.bfloat16),
            pltpu.SemaphoreType.DMA((2,)),
        ],
        compiler_params=pltpu.CompilerParams(vmem_limit_bytes=20 * 2**20),
        cost_estimate=pl.CostEstimate(
            flops=2 * pairs * k * LANES * tiles, bytes_accessed=2 * tiles * k * LANES, transcendentals=0
        ),
        name="ladder_rows",
    )(index, own, over, beyond, weights)


def pack_kernel(ladder_ref, out_ref, rest):
    devices = out_ref.shape[0] // (VIRT * MSG)
    tile = ROWS * TILES
    row = devices * tile

    def widest(step, so_far):
        return jnp.maximum(so_far, jnp.abs(ladder_ref[pl.ds(pl.multiple_of(step * tile, TILES), tile), :]))

    largest = lax.fori_loop(0, ROWS * devices, widest, jnp.zeros((tile, LANES), jnp.float32), unroll=4)
    largest = jnp.maximum(jnp.max(jnp.max(largest, axis=0, keepdims=True), axis=1, keepdims=True), 1e-30)
    power = 14.0 - jnp.ceil(jnp.log2(jnp.broadcast_to(largest, (2, LANES))))
    scale = jnp.exp2(power)[:1]

    @pl.loop(0, devices // 8)
    def _(octet):
        for half in range(2):
            first = (ROWS - 1) * (row + TILES) + half * 8
            parts = [ladder_ref[pl.ds(octet * 8 * tile + first + n, 8, stride=tile), :] for n in range(8)]
            for v, part in enumerate(exchange_groups(parts)):
                rest[pl.ds(octet * 8 * TILES + 2 * v + half, 8, stride=TILES), :] = part

    @pl.loop(0, devices, unroll=2)
    def _(device):
        first = pl.multiple_of(device * tile, TILES)
        parts = [
            ladder_ref[pl.ds(first + (k // ROWS) * row + (k % ROWS) * TILES, TILES), :] * scale for k in range(8)
        ]
        last = rest[pl.ds(pl.multiple_of(device * TILES, TILES), TILES), :] * scale
        pieces = []
        for v, part in enumerate(exchange_groups(parts)):
            pieces += [part, last[2 * v : 2 * v + 2], power]
        out_ref[pl.ds(pl.multiple_of(device * VIRT * MSG, TILES), VIRT * MSG), :] = jnp.concatenate(pieces, axis=0)


def pack(ladder):
    rows = ladder.shape[0]
    vmem = pl.BlockSpec(memory_space=pltpu.VMEM)
    return pl.pallas_call(
        pack_kernel,
        out_shape=jax.ShapeDtypeStruct((rows // VALUES * MSG, LANES), jnp.float32),
        in_specs=[vmem],
        out_specs=vmem,
        scratch_shapes=[pltpu.VMEM((rows // (ROWS * ROWS), LANES), jnp.float32)],
        compiler_params=pltpu.CompilerParams(vmem_limit_bytes=12 * 2**20),
        cost_estimate=pl.CostEstimate(flops=rows * LANES * 32, bytes_accessed=rows * LANES * 8, transcendentals=0),
        name="pack",
    )(ladder)


def finish_kernel(got_ref, *refs):
    count = (len(refs) - 3) // 2
    own_refs, factor_refs = refs[:count], refs[count : 2 * count]
    out_ref, rest, turned = refs[2 * count :]
    begin = 0
    for own_ref, factor_ref in zip(own_refs, factor_refs):
        devices = own_ref.shape[1] // ROWS

        def store(i, j, partner, begin=begin, own_ref=own_ref, factor_ref=factor_ref):
            out_ref[i, begin * ROWS + j] = (own_ref[i, j] + partner * factor_ref[i, j]).astype(out_ref.dtype)

        @pl.loop(0, devices, unroll=2)
        def _(device, begin=begin, store=store):
            first = pl.multiple_of((begin + device) * VIRT * MSG, TILES)
            block = got_ref[pl.ds(first, VIRT * MSG), :].astype(jnp.float32)
            cut = [block[v * MSG : (v + 1) * MSG] for v in range(VIRT)]
            cut = [c[:VALUES] * jnp.exp2(-c[VALUES : VALUES + 1]) for c in cut]
            main = jnp.concatenate([c[:TILES] for c in cut], axis=0).T
            rest[pl.ds(pl.multiple_of(device * TILES, TILES), TILES), :] = jnp.concatenate(
                [c[TILES:] for c in cut], axis=0
            )
            for k in range(8):
                store(k % ROWS, device * ROWS + k // ROWS, main[k * TILES : (k + 1) * TILES])

        @pl.loop(0, devices // 8)
        def _(octet, store=store):
            for half in range(2):
                parts = [rest[pl.ds(octet * 8 * TILES + 2 * v + half, 8, stride=TILES), :] for v in range(VIRT)]
                for n, part in enumerate(exchange_groups(parts)):
                    turned[pl.ds(half * 8 + n, 8, stride=TILES), :] = part
            columns = turned[...].T
            parts = [columns[v * TILES : (v + 1) * TILES] for v in range(VIRT)]
            for n, part in enumerate(exchange_groups(parts)):
                store(ROWS - 1, (octet * 8 + n) * ROWS + ROWS - 1, part)

        begin += devices


def finish(got, owns, factors):
    partners = sum(own.shape[1] for own in owns)
    vmem = pl.BlockSpec(memory_space=pltpu.VMEM)
    return pl.pallas_call(
        finish_kernel,
        out_shape=jax.ShapeDtypeStruct((ROWS, partners, TILES, LANES), jnp.bfloat16),
        in_specs=[vmem] * (1 + 2 * len(owns)),
        out_specs=vmem,
        scratch_shapes=[
            pltpu.VMEM((got.shape[0] // MSG * 2, LANES), jnp.float32),
            pltpu.VMEM((LANES, LANES), jnp.float32),
        ],
        compiler_params=pltpu.CompilerParams(vmem_limit_bytes=12 * 2**20),
        cost_estimate=pl.CostEstimate(flops=2**25, bytes_accessed=2**23, transcendentals=0),
        name="finish",
    )(got, *owns, *factors)


def after_kernel(x_ref, first_ref, out_ref):
    out_ref[...] = x_ref[...]


def after(x, first):
    vmem = pl.BlockSpec(memory_space=pltpu.VMEM)
    return pl.pallas_call(
        after_kernel,
        out_shape=jax.ShapeDtypeStruct(x.shape, x.dtype),
        in_specs=[vmem, vmem],
        out_specs=vmem,
        compiler_params=pltpu.CompilerParams(vmem_limit_bytes=4 * 2**20),
        name="after",
    )(x, first)


CHUNKS = (8, 8, 8, 8)


def per_device(amplitudes, integrals, cd_tiles, tile_counts, eps_occ, eps_virt):
    rows, partners, tiles, depth = amplitudes.shape
    slots = integrals.shape[1]
    me = lax.axis_index("virt")
    swap = [(v, v ^ 1) for v in range(VIRT)]
    relay = [(v, v + 2) for v in range(0, VIRT - 2, 2)] + [(v, v - 2) for v in range(3, VIRT, 2)]
    own, begin = [], 0
    for devices in CHUNKS:
        part = amplitudes[:, begin * rows : (begin + devices) * rows]
        own.append(jnp.transpose(part, (2, 0, 1, 3)).reshape(tiles, rows * rows * devices, depth))
        begin += devices
    over, beyond = [], []
    for n in range(len(own)):
        if n >= 2:
            own[n] = after(own[n], over[n - 2])
        over.append(lax.ppermute(own[n], "virt", swap))
    for x in over:
        beyond.append(lax.ppermute(x, "virt", relay))

    live = lax.broadcasted_iota(jnp.int32, cd_tiles.shape, 1) < tile_counts[:, None]
    block = cd_tiles // tiles - me
    over_block = jnp.where(me % 2 == 0, 1, -1)
    place = jnp.where(block == 0, 0, jnp.where(block == over_block, 1, 2))
    index = jnp.where(live, place * tiles + cd_tiles % tiles, 3 * tiles).astype(jnp.int32)

    weights = integrals.reshape(tiles, slots * depth, LANES)
    ladders = [ladder_rows(index, *parts, weights) for parts in zip(own, over, beyond)]
    sent = jnp.zeros((partners // rows * VIRT * MSG, LANES), jnp.float16)
    begin = 0
    for devices, ladder in zip(CHUNKS, ladders):
        sent = lax.dynamic_update_slice(sent, pack(ladder).astype(jnp.float16), (begin * VIRT * MSG, 0))
        begin += devices
    sent = sent.reshape(-1, MSG // 2, 2, LANES)
    got = lax.all_to_all(sent, ("pair", "virt"), split_axis=0, concat_axis=0, tiled=True)
    own_occ = lax.dynamic_slice_in_dim(eps_occ, lax.axis_index("pair") * rows, rows)
    own_virt = lax.dynamic_slice_in_dim(eps_virt, me * tiles, tiles)
    owns, factors, begin = [], [], 0
    for devices, ladder in zip(CHUNKS, ladders):
        denominator = (
            own_occ[:, None, None, None]
            + eps_occ[None, begin * rows : (begin + devices) * rows, None, None]
            - own_virt[None, None, :, None]
            - eps_virt[None, None, None, :]
        )
        owns.append(ladder.reshape(rows, rows * devices, tiles, LANES) / denominator)
        factors.append(1.0 / denominator)
        begin += devices
    return finish(got.reshape(-1, LANES).astype(jnp.float32), owns, factors)


def solution(mesh):
    in_specs = (
        P("pair", None, "virt", None),
        P("virt", None, None, None),
        P("virt", None),
        P("virt"),
        P(),
        P(),
    )
    out_specs = P("pair", None, "virt", None)
    return jax.shard_map(
        per_device, mesh=mesh, in_specs=in_specs, out_specs=out_specs, check_vma=False
    )
```

```python
import functools

import jax
import jax.numpy as jnp
from jax import lax
from jax.experimental import pallas as pl
from jax.experimental.pallas import tpu as pltpu
from jax.sharding import PartitionSpec as P

ROWS = 3
TILES = 16
VIRT = 8
LANES = 128
VALUES = ROWS * ROWS * TILES * TILES // LANES
MSG = VALUES + 2


def exchange_groups(parts):
    parts = list(parts)
    group = lax.broadcasted_iota(jnp.int32, parts[0].shape, 1) // TILES
    for step in (1, 2, 4):
        upper = (group & step) != 0
        for p in range(8):
            if p & step:
                continue
            low, high = parts[p], parts[p + step]
            parts[p] = jnp.where(upper, pltpu.roll(high, TILES * step, 1), low)
            parts[p + step] = jnp.where(upper, high, pltpu.roll(low, LANES - TILES * step, 1))
    return parts


def ladder_kernel(pieces, index_ref, *refs):
    own_ref, over_refs, next_refs = refs[0], refs[1 : 1 + pieces], refs[1 + pieces : 1 + 2 * pieces]
    ladder_body(index_ref, own_ref, over_refs, next_refs, *refs[1 + 2 * pieces :])


def ladder_body(index_ref, own_ref, over_refs, next_refs, weight_ref, out_ref, held, weights, arrived):
    group = weights.shape[1]
    slots = weight_ref.shape[1] // LANES

    def fetch(step):
        return pltpu.make_async_copy(
            weight_ref.at[pl.ds(step * group, group)], weights.at[step % 2], arrived.at[step % 2]
        )

    fetch(0).start()
    held[0:TILES] = own_ref[...]
    for n, (over_ref, next_ref) in enumerate(zip(over_refs, next_refs)):
        count = over_ref.shape[0]
        held[TILES + n * count : TILES + (n + 1) * count] = over_ref[...]
        held[2 * TILES + n * count : 2 * TILES + (n + 1) * count] = next_ref[...]
    held[3 * TILES] = jnp.zeros_like(held[3 * TILES])
    for step in range(TILES // group):
        if step + 1 < TILES // group:
            fetch(step + 1).start()
        fetch(step).wait()
        for n in range(group):
            a = step * group + n
            row = None
            for s in range(0, slots, 4):
                four = jnp.concatenate([held[index_ref[a, s + t]] for t in range(4)], axis=1)
                part = weights[step % 2, n, s * LANES : (s + 4) * LANES]
                term = jnp.dot(four, part, preferred_element_type=jnp.float32)
                row = term if row is None else row + term
            out_ref[pl.ds(a, row.shape[0], stride=TILES), :] = row


def ladder_rows(index, own, over, beyond, weights):
    tiles, pairs, depth = own.shape
    k = weights.shape[1]
    group = 4
    smem, vmem = pl.BlockSpec(memory_space=pltpu.SMEM), pl.BlockSpec(memory_space=pltpu.VMEM)
    return pl.pallas_call(
        functools.partial(ladder_kernel, len(over)),
        out_shape=jax.ShapeDtypeStruct((pairs * tiles, LANES), jnp.float32),
        in_specs=[smem] + [vmem] * (1 + 2 * len(over)) + [pl.BlockSpec(memory_space=pl.ANY)],
        out_specs=vmem,
        scratch_shapes=[
            pltpu.VMEM((3 * tiles + 1, pairs, depth), jnp.bfloat16),
            pltpu.VMEM((2, group, k, LANES), jnp.bfloat16),
            pltpu.SemaphoreType.DMA((2,)),
        ],
        compiler_params=pltpu.CompilerParams(vmem_limit_bytes=48 * 2**20),
        cost_estimate=pl.CostEstimate(
            flops=2 * pairs * k * LANES * tiles, bytes_accessed=2 * tiles * k * LANES, transcendentals=0
        ),
        name="ladder_rows",
    )(index, own, *over, *beyond, weights)


def pack_kernel(ladder_ref, out_ref, rest):
    devices = out_ref.shape[0] // (VIRT * MSG)
    tile = ROWS * TILES
    row = devices * tile

    def widest(step, so_far):
        return jnp.maximum(so_far, jnp.abs(ladder_ref[pl.ds(pl.multiple_of(step * tile, TILES), tile), :]))

    largest = lax.fori_loop(0, ROWS * devices, widest, jnp.zeros((tile, LANES), jnp.float32), unroll=4)
    largest = jnp.maximum(jnp.max(jnp.max(largest, axis=0, keepdims=True), axis=1, keepdims=True), 1e-30)
    power = 14.0 - jnp.ceil(jnp.log2(jnp.broadcast_to(largest, (2, LANES))))
    scale = jnp.exp2(power)[:1]

    @pl.loop(0, devices // 8)
    def _(octet):
        for half in range(2):
            first = (ROWS - 1) * (row + TILES) + half * 8
            parts = [ladder_ref[pl.ds(octet * 8 * tile + first + n, 8, stride=tile), :] for n in range(8)]
            for v, part in enumerate(exchange_groups(parts)):
                rest[pl.ds(octet * 8 * TILES + 2 * v + half, 8, stride=TILES), :] = part

    @pl.loop(0, devices, unroll=2)
    def _(device):
        first = pl.multiple_of(device * tile, TILES)
        parts = [
            ladder_ref[pl.ds(first + (k // ROWS) * row + (k % ROWS) * TILES, TILES), :] * scale for k in range(8)
        ]
        last = rest[pl.ds(pl.multiple_of(device * TILES, TILES), TILES), :] * scale
        pieces = []
        for v, part in enumerate(exchange_groups(parts)):
            pieces += [part, last[2 * v : 2 * v + 2], power]
        out_ref[pl.ds(pl.multiple_of(device * VIRT * MSG, TILES), VIRT * MSG), :] = jnp.concatenate(pieces, axis=0)


def pack(ladder):
    rows = ladder.shape[0]
    vmem = pl.BlockSpec(memory_space=pltpu.VMEM)
    return pl.pallas_call(
        pack_kernel,
        out_shape=jax.ShapeDtypeStruct((rows // VALUES * MSG, LANES), jnp.float32),
        in_specs=[vmem],
        out_specs=vmem,
        scratch_shapes=[pltpu.VMEM((rows // (ROWS * ROWS), LANES), jnp.float32)],
        compiler_params=pltpu.CompilerParams(vmem_limit_bytes=12 * 2**20),
        cost_estimate=pl.CostEstimate(flops=rows * LANES * 32, bytes_accessed=rows * LANES * 8, transcendentals=0),
        name="pack",
    )(ladder)


def finish_kernel(got_ref, own_ref, factor_ref, out_ref, rest, turned):
    def store(i, j, partner):
        out_ref[i, j] = (own_ref[i, j] + partner * factor_ref[i, j]).astype(out_ref.dtype)

    for device in range(8):
        block = got_ref[device * VIRT * MSG : (device + 1) * VIRT * MSG, :]
        cut = [block[v * MSG : (v + 1) * MSG] for v in range(VIRT)]
        cut = [c[:VALUES] * jnp.exp2(-c[VALUES : VALUES + 1]) for c in cut]
        main = jnp.concatenate([c[:TILES] for c in cut], axis=0).T
        rest[device * TILES : (device + 1) * TILES, :] = jnp.concatenate([c[TILES:] for c in cut], axis=0)
        for k in range(8):
            store(k % ROWS, device * ROWS + k // ROWS, main[k * TILES : (k + 1) * TILES])
    for half in range(2):
        parts = [rest[pl.ds(2 * v + half, 8, stride=TILES), :] for v in range(VIRT)]
        for n, part in enumerate(exchange_groups(parts)):
            turned[pl.ds(half * 8 + n, 8, stride=TILES), :] = part
    columns = turned[...].T
    parts = [columns[v * TILES : (v + 1) * TILES] for v in range(VIRT)]
    for n, part in enumerate(exchange_groups(parts)):
        store(ROWS - 1, n * ROWS + ROWS - 1, part)


def finish(got, own, factor):
    rows, partners = own.shape[:2]
    tile = pl.BlockSpec((rows, 8 * rows, TILES, LANES), lambda g: (0, g, 0, 0))
    return pl.pallas_call(
        finish_kernel,
        out_shape=jax.ShapeDtypeStruct(own.shape, jnp.bfloat16),
        grid=(partners // (8 * rows),),
        in_specs=[pl.BlockSpec((8 * VIRT * MSG, LANES), lambda g: (g, 0)), tile, tile],
        out_specs=tile,
        scratch_shapes=[pltpu.VMEM((8 * TILES, LANES), jnp.float32), pltpu.VMEM((LANES, LANES), jnp.float32)],
        compiler_params=pltpu.CompilerParams(vmem_limit_bytes=12 * 2**20),
        cost_estimate=pl.CostEstimate(flops=2**25, bytes_accessed=2**23, transcendentals=0),
        name="finish",
    )(got, own, factor)


def after_kernel(x_ref, first_ref, out_ref):
    out_ref[...] = x_ref[...]


def after(x, first):
    vmem = pl.BlockSpec(memory_space=pltpu.VMEM)
    return pl.pallas_call(
        after_kernel,
        out_shape=jax.ShapeDtypeStruct(x.shape, x.dtype),
        in_specs=[vmem, vmem],
        out_specs=vmem,
        compiler_params=pltpu.CompilerParams(vmem_limit_bytes=4 * 2**20),
        name="after",
    )(x, first)


CHUNKS = (16, 8, 8)
PIECES = (2, 1, 1)


def per_device(amplitudes, integrals, cd_tiles, tile_counts, eps_occ, eps_virt):
    rows, partners, tiles, depth = amplitudes.shape
    slots = integrals.shape[1]
    me = lax.axis_index("virt")
    swap = [(v, v ^ 1) for v in range(VIRT)]
    relay = [(v, v + 2) for v in range(0, VIRT - 2, 2)] + [(v, v - 2) for v in range(3, VIRT, 2)]
    own, begin = [], 0
    for devices in CHUNKS:
        part = amplitudes[:, begin * rows : (begin + devices) * rows]
        own.append(jnp.transpose(part, (2, 0, 1, 3)).reshape(tiles, rows * rows * devices, depth))
        begin += devices
    over, beyond, order = [], [], []
    for part, pieces in zip(own, PIECES):
        count = tiles // pieces
        over.append([])
        for n in range(pieces):
            piece = part[n * count : (n + 1) * count]
            if len(order) >= 2:
                piece = after(piece, order[-2])
            order.append(lax.ppermute(piece, "virt", swap))
            over[-1].append(order[-1])
    beyond = [[lax.ppermute(x, "virt", relay) for x in group] for group in over]

    live = lax.broadcasted_iota(jnp.int32, cd_tiles.shape, 1) < tile_counts[:, None]
    block = cd_tiles // tiles - me
    over_block = jnp.where(me % 2 == 0, 1, -1)
    place = jnp.where(block == 0, 0, jnp.where(block == over_block, 1, 2))
    index = jnp.where(live, place * tiles + cd_tiles % tiles, 3 * tiles).astype(jnp.int32)

    weights = integrals.reshape(tiles, slots * depth, LANES)
    ladders = [ladder_rows(index, *parts, weights) for parts in zip(own, over, beyond)]
    sent = jnp.zeros((partners // rows * VIRT * MSG, LANES), jnp.float16)
    begin = 0
    for devices, ladder in zip(CHUNKS, ladders):
        sent = lax.dynamic_update_slice(sent, pack(ladder).astype(jnp.float16), (begin * VIRT * MSG, 0))
        begin += devices
    sent = sent.reshape(-1, MSG // 2, 2, LANES)
    got = lax.all_to_all(sent, ("pair", "virt"), split_axis=0, concat_axis=0, tiled=True)
    own_occ = lax.dynamic_slice_in_dim(eps_occ, lax.axis_index("pair") * rows, rows)
    own_virt = lax.dynamic_slice_in_dim(eps_virt, me * tiles, tiles)
    denominator = (
        own_occ[:, None, None, None]
        + eps_occ[None, :, None, None]
        - own_virt[None, None, :, None]
        - eps_virt[None, None, None, :]
    )
    ladder = jnp.concatenate([x.reshape(rows, -1, tiles, LANES) for x in ladders], axis=1)
    return finish(got.reshape(-1, LANES).astype(jnp.float32), ladder / denominator, 1.0 / denominator)


def solution(mesh):
    in_specs = (
        P("pair", None, "virt", None),
        P("virt", None, None, None),
        P("virt", None),
        P("virt"),
        P(),
        P(),
    )
    out_specs = P("pair", None, "virt", None)
    return jax.shard_map(
        per_device, mesh=mesh, in_specs=in_specs, out_specs=out_specs, check_vma=False
    )
```

```python
import functools

import jax
import jax.numpy as jnp
from jax import lax
from jax.experimental import pallas as pl
from jax.experimental.pallas import tpu as pltpu
from jax.sharding import PartitionSpec as P

ROWS = 3
TILES = 16
VIRT = 8
LANES = 128
VALUES = ROWS * ROWS * TILES * TILES // LANES
MSG = VALUES + 2


def exchange_groups(parts):
    parts = list(parts)
    group = lax.broadcasted_iota(jnp.int32, parts[0].shape, 1) // TILES
    for step in (1, 2, 4):
        upper = (group & step) != 0
        for p in range(8):
            if p & step:
                continue
            low, high = parts[p], parts[p + step]
            parts[p] = jnp.where(upper, pltpu.roll(high, TILES * step, 1), low)
            parts[p + step] = jnp.where(upper, high, pltpu.roll(low, LANES - TILES * step, 1))
    return parts


def ladder_kernel(pieces, index_ref, own_ref, *refs):
    over_refs, next_refs = refs[:pieces], refs[pieces : 2 * pieces]
    weight_ref, out_ref, held, weights, arrived = refs[2 * pieces :]
    slots = weight_ref.shape[1] // LANES

    def fetch(a):
        return pltpu.make_async_copy(weight_ref.at[a], weights.at[a], arrived.at[a])

    for a in range(TILES):
        fetch(a).start()
    held[0:TILES] = own_ref[...]
    for n, (over_ref, next_ref) in enumerate(zip(over_refs, next_refs)):
        count = over_ref.shape[0]
        held[TILES + n * count : TILES + (n + 1) * count] = over_ref[...]
        held[2 * TILES + n * count : 2 * TILES + (n + 1) * count] = next_ref[...]
    held[3 * TILES] = jnp.zeros_like(held[3 * TILES])

    @pl.loop(0, TILES // 4)
    def _(step):
        for n in range(4):
            a = step * 4 + n
            fetch(a).wait()
            row = None
            for s in range(0, slots, 4):
                four = jnp.concatenate([held[index_ref[a, s + t]] for t in range(4)], axis=1)
                part = weights[a, s * LANES : (s + 4) * LANES]
                term = jnp.dot(four, part, preferred_element_type=jnp.float32)
                row = term if row is None else row + term
            out_ref[pl.ds(a, row.shape[0], stride=TILES), :] = row


def ladder_rows(index, own, over, beyond, weights):
    tiles, pairs, depth = own.shape
    k = weights.shape[1]
    smem, vmem = pl.BlockSpec(memory_space=pltpu.SMEM), pl.BlockSpec(memory_space=pltpu.VMEM)
    return pl.pallas_call(
        functools.partial(ladder_kernel, len(over)),
        out_shape=jax.ShapeDtypeStruct((pairs * tiles, LANES), jnp.float32),
        in_specs=[smem] + [vmem] * (1 + 2 * len(over)) + [pl.BlockSpec(memory_space=pl.ANY)],
        out_specs=vmem,
        scratch_shapes=[
            pltpu.VMEM((3 * tiles + 1, pairs, depth), jnp.bfloat16),
            pltpu.VMEM(weights.shape, jnp.bfloat16),
            pltpu.SemaphoreType.DMA((tiles,)),
        ],
        compiler_params=pltpu.CompilerParams(vmem_limit_bytes=48 * 2**20),
        cost_estimate=pl.CostEstimate(
            flops=2 * pairs * k * LANES * tiles, bytes_accessed=2 * tiles * k * LANES, transcendentals=0
        ),
        name="ladder_rows",
    )(index, own, *over, *beyond, weights)


def pack_kernel(ladder_ref, out_ref, rest):
    devices = out_ref.shape[0] // (VIRT * MSG)
    tile = ROWS * TILES
    row = devices * tile

    def widest(step, so_far):
        return jnp.maximum(so_far, jnp.abs(ladder_ref[pl.ds(pl.multiple_of(step * tile, TILES), tile), :]))

    largest = lax.fori_loop(0, ROWS * devices, widest, jnp.zeros((tile, LANES), jnp.float32), unroll=4)
    largest = jnp.maximum(jnp.max(jnp.max(largest, axis=0, keepdims=True), axis=1, keepdims=True), 1e-30)
    power = 14.0 - jnp.ceil(jnp.log2(jnp.broadcast_to(largest, (2, LANES))))
    scale = jnp.exp2(power)[:1]

    @pl.loop(0, devices // 8)
    def _(octet):
        for half in range(2):
            first = (ROWS - 1) * (row + TILES) + half * 8
            parts = [ladder_ref[pl.ds(octet * 8 * tile + first + n, 8, stride=tile), :] for n in range(8)]
            for v, part in enumerate(exchange_groups(parts)):
                rest[pl.ds(octet * 8 * TILES + 2 * v + half, 8, stride=TILES), :] = part

    @pl.loop(0, devices, unroll=2)
    def _(device):
        first = pl.multiple_of(device * tile, TILES)
        parts = [
            ladder_ref[pl.ds(first + (k // ROWS) * row + (k % ROWS) * TILES, TILES), :] * scale for k in range(8)
        ]
        last = rest[pl.ds(pl.multiple_of(device * TILES, TILES), TILES), :] * scale
        pieces = []
        for v, part in enumerate(exchange_groups(parts)):
            pieces += [part, last[2 * v : 2 * v + 2], power]
        out_ref[pl.ds(pl.multiple_of(device * VIRT * MSG, TILES), VIRT * MSG), :] = jnp.concatenate(pieces, axis=0)


def pack(ladder):
    rows = ladder.shape[0]
    vmem = pl.BlockSpec(memory_space=pltpu.VMEM)
    return pl.pallas_call(
        pack_kernel,
        out_shape=jax.ShapeDtypeStruct((rows // VALUES * MSG, LANES), jnp.float32),
        in_specs=[vmem],
        out_specs=vmem,
        scratch_shapes=[pltpu.VMEM((rows // (ROWS * ROWS), LANES), jnp.float32)],
        compiler_params=pltpu.CompilerParams(vmem_limit_bytes=12 * 2**20),
        cost_estimate=pl.CostEstimate(flops=rows * LANES * 32, bytes_accessed=rows * LANES * 8, transcendentals=0),
        name="pack",
    )(ladder)


def finish_kernel(got_ref, own_ref, factor_ref, out_ref, rest, turned):
    def store(i, j, partner):
        out_ref[i, j] = (own_ref[i, j] + partner * factor_ref[i, j]).astype(out_ref.dtype)

    for device in range(8):
        block = got_ref[device * VIRT * MSG : (device + 1) * VIRT * MSG, :]
        cut = [block[v * MSG : (v + 1) * MSG] for v in range(VIRT)]
        cut = [c[:VALUES] * jnp.exp2(-c[VALUES : VALUES + 1]) for c in cut]
        main = jnp.concatenate([c[:TILES] for c in cut], axis=0).T
        rest[device * TILES : (device + 1) * TILES, :] = jnp.concatenate([c[TILES:] for c in cut], axis=0)
        for k in range(8):
            store(k % ROWS, device * ROWS + k // ROWS, main[k * TILES : (k + 1) * TILES])
    for half in range(2):
        parts = [rest[pl.ds(2 * v + half, 8, stride=TILES), :] for v in range(VIRT)]
        for n, part in enumerate(exchange_groups(parts)):
            turned[pl.ds(half * 8 + n, 8, stride=TILES), :] = part
    columns = turned[...].T
    parts = [columns[v * TILES : (v + 1) * TILES] for v in range(VIRT)]
    for n, part in enumerate(exchange_groups(parts)):
        store(ROWS - 1, n * ROWS + ROWS - 1, part)


def finish(got, own, factor):
    rows, partners = own.shape[:2]
    tile = pl.BlockSpec((rows, 8 * rows, TILES, LANES), lambda g: (0, g, 0, 0))
    return pl.pallas_call(
        finish_kernel,
        out_shape=jax.ShapeDtypeStruct(own.shape, jnp.bfloat16),
        grid=(partners // (8 * rows),),
        in_specs=[pl.BlockSpec((8 * VIRT * MSG, LANES), lambda g: (g, 0)), tile, tile],
        out_specs=tile,
        scratch_shapes=[pltpu.VMEM((8 * TILES, LANES), jnp.float32), pltpu.VMEM((LANES, LANES), jnp.float32)],
        compiler_params=pltpu.CompilerParams(vmem_limit_bytes=12 * 2**20),
        cost_estimate=pl.CostEstimate(flops=2**25, bytes_accessed=2**23, transcendentals=0),
        name="finish",
    )(got, own, factor)


def after_kernel(x_ref, *refs):
    refs[-1][...] = x_ref[...]


def after(x, *first):
    vmem = pl.BlockSpec(memory_space=pltpu.VMEM)
    return pl.pallas_call(
        after_kernel,
        out_shape=jax.ShapeDtypeStruct(x.shape, x.dtype),
        in_specs=[vmem] * (1 + len(first)),
        out_specs=vmem,
        compiler_params=pltpu.CompilerParams(vmem_limit_bytes=12 * 2**20),
        name="after",
    )(x, *first)


CHUNKS = (16, 8, 8)


def per_device(amplitudes, integrals, cd_tiles, tile_counts, eps_occ, eps_virt):
    rows, partners, tiles, depth = amplitudes.shape
    slots = integrals.shape[1]
    me = lax.axis_index("virt")
    swap = [(v, v ^ 1) for v in range(VIRT)]
    relay = [(v, v + 2) for v in range(0, VIRT - 2, 2)] + [(v, v - 2) for v in range(3, VIRT, 2)]
    own, begin = [], 0
    for devices in CHUNKS:
        part = amplitudes[:, begin * rows : (begin + devices) * rows]
        own.append(jnp.transpose(part, (2, 0, 1, 3)).reshape(tiles, rows * rows * devices, depth))
        begin += devices
    live = lax.broadcasted_iota(jnp.int32, cd_tiles.shape, 1) < tile_counts[:, None]
    block = cd_tiles // tiles - me
    over_block = jnp.where(me % 2 == 0, 1, -1)
    place = jnp.where(block == 0, 0, jnp.where(block == over_block, 1, 2))
    index = jnp.where(live, place * tiles + cd_tiles % tiles, 3 * tiles).astype(jnp.int32)

    weights = integrals.reshape(tiles, slots * depth, LANES)

    def swapped(x):
        return lax.ppermute(x, "virt", swap)

    def passed_on(x):
        return lax.ppermute(x, "virt", relay)

    half = tiles // 2
    over_a = [swapped(own[0][:half]), swapped(own[0][half:])]
    own[1] = after(own[1], over_a[0])
    over_b = swapped(own[1])
    beyond_a = [passed_on(x) for x in over_a]
    own[2] = after(own[2], over_a[1], beyond_a[0])
    over_c = swapped(own[2])
    beyond_b = passed_on(over_b)
    ladder_a = ladder_rows(index, own[0], over_a, beyond_a, weights)
    beyond_c = passed_on(after(over_c, ladder_a))
    ladder_b = ladder_rows(index, own[1], [over_b], [beyond_b], weights)
    ladder_c = ladder_rows(index, own[2], [over_c], [beyond_c], weights)
    ladders = [ladder_a, ladder_b, ladder_c]
    sent = jnp.zeros((partners // rows * VIRT * MSG, LANES), jnp.float16)
    begin = 0
    for devices, ladder in zip(CHUNKS, ladders):
        sent = lax.dynamic_update_slice(sent, pack(ladder).astype(jnp.float16), (begin * VIRT * MSG, 0))
        begin += devices
    sent = sent.reshape(-1, MSG // 2, 2, LANES)
    got = lax.all_to_all(sent, ("pair", "virt"), split_axis=0, concat_axis=0, tiled=True)
    own_occ = lax.dynamic_slice_in_dim(eps_occ, lax.axis_index("pair") * rows, rows)
    own_virt = lax.dynamic_slice_in_dim(eps_virt, me * tiles, tiles)
    denominator = (
        own_occ[:, None, None, None]
        + eps_occ[None, :, None, None]
        - own_virt[None, None, :, None]
        - eps_virt[None, None, None, :]
    )
    ladder = jnp.concatenate([x.reshape(rows, -1, tiles, LANES) for x in ladders], axis=1)
    return finish(got.reshape(-1, LANES).astype(jnp.float32), ladder / denominator, 1.0 / denominator)


def solution(mesh):
    in_specs = (
        P("pair", None, "virt", None),
        P("virt", None, None, None),
        P("virt", None),
        P("virt"),
        P(),
        P(),
    )
    out_specs = P("pair", None, "virt", None)
    return jax.shard_map(
        per_device, mesh=mesh, in_specs=in_specs, out_specs=out_specs, check_vma=False
    )
```

```python
import functools

import jax
import jax.numpy as jnp
from jax import lax
from jax.experimental import pallas as pl
from jax.experimental.pallas import tpu as pltpu
from jax.sharding import PartitionSpec as P

ROWS = 3
TILES = 16
VIRT = 8
LANES = 128
VALUES = ROWS * ROWS * TILES * TILES // LANES
MSG = VALUES + 2


def exchange_groups(parts):
    parts = list(parts)
    group = lax.broadcasted_iota(jnp.int32, parts[0].shape, 1) // TILES
    for step in (1, 2, 4):
        upper = (group & step) != 0
        for p in range(8):
            if p & step:
                continue
            low, high = parts[p], parts[p + step]
            parts[p] = jnp.where(upper, pltpu.roll(high, TILES * step, 1), low)
            parts[p + step] = jnp.where(upper, high, pltpu.roll(low, LANES - TILES * step, 1))
    return parts


def ladder_kernel(pieces, index_ref, own_ref, *refs):
    over_refs, next_refs = refs[:pieces], refs[pieces : 2 * pieces]
    weight_ref, out_ref, held, weights, arrived = refs[2 * pieces :]
    slots = weight_ref.shape[1] // LANES

    def fetch(a):
        return pltpu.make_async_copy(weight_ref.at[a], weights.at[a], arrived.at[a])

    for a in range(4):
        fetch(a).start()
    held[0:TILES] = own_ref[...]
    for n, (over_ref, next_ref) in enumerate(zip(over_refs, next_refs)):
        count = over_ref.shape[0]
        held[TILES + n * count : TILES + (n + 1) * count] = over_ref[...]
        held[2 * TILES + n * count : 2 * TILES + (n + 1) * count] = next_ref[...]
    held[3 * TILES] = jnp.zeros_like(held[3 * TILES])

    @pl.loop(0, TILES // 4)
    def _(step):
        for n in range(4):
            a = step * 4 + n
            fetch(a).wait()

            @pl.when(a + 4 < TILES)
            def _(a=a):
                fetch(a + 4).start()

            row = None
            for s in range(0, slots, 4):
                four = jnp.concatenate([held[index_ref[a, s + t]] for t in range(4)], axis=1)
                part = weights[a, s * LANES : (s + 4) * LANES]
                term = jnp.dot(four, part, preferred_element_type=jnp.float32)
                row = term if row is None else row + term
            out_ref[pl.ds(a, row.shape[0], stride=TILES), :] = row


def ladder_rows(index, own, over, beyond, weights):
    tiles, pairs, depth = own.shape
    k = weights.shape[1]
    smem, vmem = pl.BlockSpec(memory_space=pltpu.SMEM), pl.BlockSpec(memory_space=pltpu.VMEM)
    return pl.pallas_call(
        functools.partial(ladder_kernel, len(over)),
        out_shape=jax.ShapeDtypeStruct((pairs * tiles, LANES), jnp.float32),
        in_specs=[smem] + [vmem] * (1 + 2 * len(over)) + [pl.BlockSpec(memory_space=pl.ANY)],
        out_specs=vmem,
        scratch_shapes=[
            pltpu.VMEM((3 * tiles + 1, pairs, depth), jnp.bfloat16),
            pltpu.VMEM(weights.shape, jnp.bfloat16),
            pltpu.SemaphoreType.DMA((tiles,)),
        ],
        compiler_params=pltpu.CompilerParams(vmem_limit_bytes=48 * 2**20),
        cost_estimate=pl.CostEstimate(
            flops=2 * pairs * k * LANES * tiles, bytes_accessed=2 * tiles * k * LANES, transcendentals=0
        ),
        name="ladder_rows",
    )(index, own, *over, *beyond, weights)


def pack_kernel(ladder_ref, *refs):
    out_ref, rest = refs[-2:]
    devices = ladder_ref.shape[0] // (VIRT * VALUES)
    begin = 0
    for earlier in refs[:-2]:
        out_ref[begin : begin + earlier.shape[0], :] = earlier[...]
        begin += earlier.shape[0]
    tile = ROWS * TILES
    row = devices * tile

    def widest(step, so_far):
        return jnp.maximum(so_far, jnp.abs(ladder_ref[pl.ds(pl.multiple_of(step * tile, TILES), tile), :]))

    largest = lax.fori_loop(0, ROWS * devices, widest, jnp.zeros((tile, LANES), jnp.float32), unroll=4)
    largest = jnp.maximum(jnp.max(jnp.max(largest, axis=0, keepdims=True), axis=1, keepdims=True), 1e-30)
    power = 14.0 - jnp.ceil(jnp.log2(jnp.broadcast_to(largest, (2, LANES))))
    scale = jnp.exp2(power)[:1]

    @pl.loop(0, devices // 8)
    def _(octet):
        for half in range(2):
            first = (ROWS - 1) * (row + TILES) + half * 8
            parts = [ladder_ref[pl.ds(octet * 8 * tile + first + n, 8, stride=tile), :] for n in range(8)]
            for v, part in enumerate(exchange_groups(parts)):
                rest[pl.ds(octet * 8 * TILES + 2 * v + half, 8, stride=TILES), :] = part

    @pl.loop(0, devices, unroll=2)
    def _(device):
        first = pl.multiple_of(device * tile, TILES)
        parts = [
            ladder_ref[pl.ds(first + (k // ROWS) * row + (k % ROWS) * TILES, TILES), :] * scale for k in range(8)
        ]
        last = rest[pl.ds(pl.multiple_of(device * TILES, TILES), TILES), :] * scale
        pieces = []
        for v, part in enumerate(exchange_groups(parts)):
            pieces += [part, last[2 * v : 2 * v + 2], power]
        place = pl.multiple_of(begin + device * VIRT * MSG, TILES)
        out_ref[pl.ds(place, VIRT * MSG), :] = jnp.concatenate(pieces, axis=0)


def pack(ladder, *earlier):
    rows = ladder.shape[0]
    before = sum(x.shape[0] for x in earlier)
    vmem = pl.BlockSpec(memory_space=pltpu.VMEM)
    return pl.pallas_call(
        pack_kernel,
        out_shape=jax.ShapeDtypeStruct((before + rows // VALUES * MSG, LANES), jnp.float32),
        in_specs=[vmem] * (1 + len(earlier)),
        out_specs=vmem,
        scratch_shapes=[pltpu.VMEM((rows // (ROWS * ROWS), LANES), jnp.float32)],
        compiler_params=pltpu.CompilerParams(vmem_limit_bytes=12 * 2**20),
        cost_estimate=pl.CostEstimate(flops=rows * LANES * 32, bytes_accessed=rows * LANES * 8, transcendentals=0),
        name="pack",
    )(ladder, *earlier)


def finish_kernel(got_ref, own_ref, factor_ref, out_ref, rest, turned):
    def store(i, j, partner):
        out_ref[i, j] = (own_ref[i, j] + partner * factor_ref[i, j]).astype(out_ref.dtype)

    for device in range(8):
        block = got_ref[device * VIRT * MSG : (device + 1) * VIRT * MSG, :]
        cut = [block[v * MSG : (v + 1) * MSG] for v in range(VIRT)]
        cut = [c[:VALUES] * jnp.exp2(-c[VALUES : VALUES + 1]) for c in cut]
        main = jnp.concatenate([c[:TILES] for c in cut], axis=0).T
        rest[device * TILES : (device + 1) * TILES, :] = jnp.concatenate([c[TILES:] for c in cut], axis=0)
        for k in range(8):
            store(k % ROWS, device * ROWS + k // ROWS, main[k * TILES : (k + 1) * TILES])
    for half in range(2):
        parts = [rest[pl.ds(2 * v + half, 8, stride=TILES), :] for v in range(VIRT)]
        for n, part in enumerate(exchange_groups(parts)):
            turned[pl.ds(half * 8 + n, 8, stride=TILES), :] = part
    columns = turned[...].T
    parts = [columns[v * TILES : (v + 1) * TILES] for v in range(VIRT)]
    for n, part in enumerate(exchange_groups(parts)):
        store(ROWS - 1, n * ROWS + ROWS - 1, part)


def finish(got, own, factor):
    rows, partners = own.shape[:2]
    tile = pl.BlockSpec((rows, 8 * rows, TILES, LANES), lambda g: (0, g, 0, 0))
    return pl.pallas_call(
        finish_kernel,
        out_shape=jax.ShapeDtypeStruct(own.shape, jnp.bfloat16),
        grid=(partners // (8 * rows),),
        in_specs=[pl.BlockSpec((8 * VIRT * MSG, LANES), lambda g: (g, 0)), tile, tile],
        out_specs=tile,
        scratch_shapes=[pltpu.VMEM((8 * TILES, LANES), jnp.float32), pltpu.VMEM((LANES, LANES), jnp.float32)],
        compiler_params=pltpu.CompilerParams(vmem_limit_bytes=12 * 2**20),
        cost_estimate=pl.CostEstimate(flops=2**25, bytes_accessed=2**23, transcendentals=0),
        name="finish",
    )(got, own, factor)


def after_kernel(x_ref, *refs):
    refs[-1][...] = x_ref[...]


def after(x, *first):
    vmem = pl.BlockSpec(memory_space=pltpu.VMEM)
    return pl.pallas_call(
        after_kernel,
        out_shape=jax.ShapeDtypeStruct(x.shape, x.dtype),
        in_specs=[vmem] * (1 + len(first)),
        out_specs=vmem,
        compiler_params=pltpu.CompilerParams(vmem_limit_bytes=12 * 2**20),
        name="after",
    )(x, *first)


CHUNKS = (16, 16)


def per_device(amplitudes, integrals, cd_tiles, tile_counts, eps_occ, eps_virt):
    rows, partners, tiles, depth = amplitudes.shape
    slots = integrals.shape[1]
    me = lax.axis_index("virt")
    swap = [(v, v ^ 1) for v in range(VIRT)]
    relay = [(v, v + 2) for v in range(0, VIRT - 2, 2)] + [(v, v - 2) for v in range(3, VIRT, 2)]
    own, begin = [], 0
    for devices in CHUNKS:
        part = amplitudes[:, begin * rows : (begin + devices) * rows]
        own.append(jnp.transpose(part, (2, 0, 1, 3)).reshape(tiles, rows * rows * devices, depth))
        begin += devices
    live = lax.broadcasted_iota(jnp.int32, cd_tiles.shape, 1) < tile_counts[:, None]
    block = cd_tiles // tiles - me
    over_block = jnp.where(me % 2 == 0, 1, -1)
    place = jnp.where(block == 0, 0, jnp.where(block == over_block, 1, 2))
    index = jnp.where(live, place * tiles + cd_tiles % tiles, 3 * tiles).astype(jnp.int32)

    weights = integrals.reshape(tiles, slots * depth, LANES)

    def swapped(x):
        return lax.ppermute(x, "virt", swap)

    def passed_on(x):
        return lax.ppermute(x, "virt", relay)

    half = tiles // 2
    over_a = [swapped(own[0][:half]), swapped(own[0][half:])]
    over_b = [swapped(after(own[1][:half], over_a[0])), swapped(after(own[1][half:], over_a[0]))]
    beyond_a = [passed_on(x) for x in over_a]
    beyond_b = [passed_on(x) for x in over_b]
    ladders = [
        ladder_rows(index, own[0], over_a, beyond_a, weights),
        ladder_rows(index, own[1], over_b, beyond_b, weights),
    ]
    sent = pack(ladders[1], pack(ladders[0])).astype(jnp.float16).reshape(-1, MSG // 2, 2, LANES)
    got = lax.all_to_all(sent, ("pair", "virt"), split_axis=0, concat_axis=0, tiled=True)
    own_occ = lax.dynamic_slice_in_dim(eps_occ, lax.axis_index("pair") * rows, rows)
    own_virt = lax.dynamic_slice_in_dim(eps_virt, me * tiles, tiles)
    denominator = (
        own_occ[:, None, None, None]
        + eps_occ[None, :, None, None]
        - own_virt[None, None, :, None]
        - eps_virt[None, None, None, :]
    )
    ladder = jnp.concatenate([x.reshape(rows, -1, tiles, LANES) for x in ladders], axis=1)
    return finish(got.reshape(-1, LANES).astype(jnp.float32), ladder / denominator, 1.0 / denominator)


def solution(mesh):
    in_specs = (
        P("pair", None, "virt", None),
        P("virt", None, None, None),
        P("virt", None),
        P("virt"),
        P(),
        P(),
    )
    out_specs = P("pair", None, "virt", None)
    return jax.shard_map(
        per_device, mesh=mesh, in_specs=in_specs, out_specs=out_specs, check_vma=False
    )
```

```python
import functools

import jax
import jax.numpy as jnp
from jax import lax
from jax.experimental import pallas as pl
from jax.experimental.pallas import tpu as pltpu
from jax.sharding import PartitionSpec as P

ROWS = 3
TILES = 16
VIRT = 8
LANES = 128
VALUES = ROWS * ROWS * TILES * TILES // LANES
MSG = VALUES + 2


def exchange_groups(parts):
    parts = list(parts)
    group = lax.broadcasted_iota(jnp.int32, parts[0].shape, 1) // TILES
    for step in (1, 2, 4):
        upper = (group & step) != 0
        for p in range(8):
            if p & step:
                continue
            low, high = parts[p], parts[p + step]
            parts[p] = jnp.where(upper, pltpu.roll(high, TILES * step, 1), low)
            parts[p + step] = jnp.where(upper, high, pltpu.roll(low, LANES - TILES * step, 1))
    return parts


GROUP = 4


def ladder_kernel(index_ref, *refs):
    weight_ref, out_ref, held, weights, landed, arrived = refs[-6:]
    slots = weight_ref.shape[1] // LANES

    def fetch(a):
        return pltpu.make_async_copy(weight_ref.at[a], weights.at[a], arrived.at[a])

    columns, begin = [], 0
    for n, ref in enumerate(refs[:-6]):
        place = held.at[pl.ds(begin, ref.shape[0])]
        columns.append(pltpu.make_async_copy(ref, place, landed.at[n]))
        begin += ref.shape[0]
    for copy in columns:
        copy.start()
    for a in range(2 * GROUP):
        fetch(a).start()
    held[3 * TILES] = jnp.zeros_like(held[3 * TILES])
    for copy in columns:
        copy.wait()
    for first in range(0, TILES, GROUP):
        for a in range(first, first + GROUP):
            fetch(a).wait()
            if a + 2 * GROUP < TILES:
                fetch(a + 2 * GROUP).start()
        for a in range(first, first + GROUP):
            row = None
            for s in range(0, slots, 4):
                four = jnp.concatenate([held[index_ref[a, s + t]] for t in range(4)], axis=1)
                part = weights[a, s * LANES : (s + 4) * LANES]
                term = jnp.dot(four, part, preferred_element_type=jnp.float32)
                row = term if row is None else row + term
            out_ref[pl.ds(a, row.shape[0], stride=TILES), :] = row


def ladder_rows(index, columns, weights):
    pairs, depth = columns[0].shape[1:]
    tiles, k = weights.shape[:2]
    anywhere = pl.BlockSpec(memory_space=pl.ANY)
    return pl.pallas_call(
        ladder_kernel,
        out_shape=jax.ShapeDtypeStruct((pairs * tiles, LANES), jnp.float32),
        in_specs=[pl.BlockSpec(memory_space=pltpu.SMEM)] + [anywhere] * (len(columns) + 1),
        out_specs=pl.BlockSpec(memory_space=pltpu.VMEM),
        scratch_shapes=[
            pltpu.VMEM((3 * tiles + 1, pairs, depth), jnp.bfloat16),
            pltpu.VMEM(weights.shape, jnp.bfloat16),
            pltpu.SemaphoreType.DMA((len(columns),)),
            pltpu.SemaphoreType.DMA((tiles,)),
        ],
        compiler_params=pltpu.CompilerParams(vmem_limit_bytes=48 * 2**20),
        cost_estimate=pl.CostEstimate(
            flops=2 * pairs * k * LANES * tiles, bytes_accessed=2 * tiles * k * LANES, transcendentals=0
        ),
        name="ladder_rows",
    )(index, *columns, weights)


def pack_kernel(ladder_ref, *refs):
    out_ref, rest = refs[-2:]
    devices = ladder_ref.shape[0] // (VIRT * VALUES)
    begin = 0
    for earlier in refs[:-2]:
        out_ref[begin : begin + earlier.shape[0], :] = earlier[...]
        begin += earlier.shape[0]
    tile = ROWS * TILES
    row = devices * tile

    def widest(step, so_far):
        return jnp.maximum(so_far, jnp.abs(ladder_ref[pl.ds(pl.multiple_of(step * tile, TILES), tile), :]))

    largest = lax.fori_loop(0, ROWS * devices, widest, jnp.zeros((tile, LANES), jnp.float32), unroll=4)
    largest = jnp.maximum(jnp.max(jnp.max(largest, axis=0, keepdims=True), axis=1, keepdims=True), 1e-30)
    power = 14.0 - jnp.ceil(jnp.log2(jnp.broadcast_to(largest, (2, LANES))))
    scale = jnp.exp2(power)[:1]

    @pl.loop(0, devices // 8)
    def _(octet):
        for half in range(2):
            first = (ROWS - 1) * (row + TILES) + half * 8
            parts = [ladder_ref[pl.ds(octet * 8 * tile + first + n, 8, stride=tile), :] for n in range(8)]
            for v, part in enumerate(exchange_groups(parts)):
                rest[pl.ds(octet * 8 * TILES + 2 * v + half, 8, stride=TILES), :] = part

    @pl.loop(0, devices, unroll=2)
    def _(device):
        first = pl.multiple_of(device * tile, TILES)
        parts = [
            ladder_ref[pl.ds(first + (k // ROWS) * row + (k % ROWS) * TILES, TILES), :] * scale for k in range(8)
        ]
        last = rest[pl.ds(pl.multiple_of(device * TILES, TILES), TILES), :] * scale
        pieces = []
        for v, part in enumerate(exchange_groups(parts)):
            pieces += [part, last[2 * v : 2 * v + 2], power]
        place = pl.multiple_of(begin + device * VIRT * MSG, TILES)
        out_ref[pl.ds(place, VIRT * MSG), :] = jnp.concatenate(pieces, axis=0)


def pack(ladder, *earlier):
    rows = ladder.shape[0]
    before = sum(x.shape[0] for x in earlier)
    vmem = pl.BlockSpec(memory_space=pltpu.VMEM)
    return pl.pallas_call(
        pack_kernel,
        out_shape=jax.ShapeDtypeStruct((before + rows // VALUES * MSG, LANES), jnp.float32),
        in_specs=[vmem] * (1 + len(earlier)),
        out_specs=vmem,
        scratch_shapes=[pltpu.VMEM((rows // (ROWS * ROWS), LANES), jnp.float32)],
        compiler_params=pltpu.CompilerParams(vmem_limit_bytes=12 * 2**20),
        cost_estimate=pl.CostEstimate(flops=rows * LANES * 32, bytes_accessed=rows * LANES * 8, transcendentals=0),
        name="pack",
    )(ladder, *earlier)


def finish_kernel(occ_ref, own_occ_ref, got_ref, first_ref, second_ref, va_ref, vb_ref, out_ref, rest, turned):
    step = pl.program_id(0)
    half = pl.num_programs(0) // 2

    def work(ladder_ref):
        def store(i, j, partner):
            bottom = (own_occ_ref[i] + occ_ref[step * 8 * ROWS + j]) - va_ref[...] - vb_ref[...]
            out_ref[i, j] = ((ladder_ref[i, j] + partner) * (1.0 / bottom)).astype(out_ref.dtype)

        for device in range(8):
            block = got_ref[device * VIRT * MSG : (device + 1) * VIRT * MSG, :]
            cut = [block[v * MSG : (v + 1) * MSG] for v in range(VIRT)]
            cut = [c[:VALUES] * jnp.exp2(-c[VALUES : VALUES + 1]) for c in cut]
            main = jnp.concatenate([c[:TILES] for c in cut], axis=0).T
            rest[device * TILES : (device + 1) * TILES, :] = jnp.concatenate([c[TILES:] for c in cut], axis=0)
            for k in range(8):
                store(k % ROWS, device * ROWS + k // ROWS, main[k * TILES : (k + 1) * TILES])
        for side in range(2):
            parts = [rest[pl.ds(2 * v + side, 8, stride=TILES), :] for v in range(VIRT)]
            for n, part in enumerate(exchange_groups(parts)):
                turned[pl.ds(side * 8 + n, 8, stride=TILES), :] = part
        columns = turned[...].T
        parts = [columns[v * TILES : (v + 1) * TILES] for v in range(VIRT)]
        for n, part in enumerate(exchange_groups(parts)):
            store(ROWS - 1, n * ROWS + ROWS - 1, part)

    @pl.when(step < half)
    def _():
        work(first_ref)

    @pl.when(step >= half)
    def _():
        work(second_ref)


def finish(occ, own_occ, got, ladders, va, vb):
    rows, partners = own_occ.shape[0], occ.shape[0]
    steps = partners // (8 * rows)
    smem = pl.BlockSpec(memory_space=pltpu.SMEM)
    shape = (rows, 8 * rows, TILES, LANES)
    first = pl.BlockSpec(shape, lambda g: (0, jnp.minimum(g, steps // 2 - 1), 0, 0))
    second = pl.BlockSpec(shape, lambda g: (0, jnp.maximum(g - steps // 2, 0), 0, 0))
    table = pl.BlockSpec((TILES, LANES), lambda g: (0, 0))
    return pl.pallas_call(
        finish_kernel,
        out_shape=jax.ShapeDtypeStruct((rows, partners, TILES, LANES), jnp.bfloat16),
        grid=(steps,),
        in_specs=[smem, smem, pl.BlockSpec((8 * VIRT * MSG, LANES), lambda g: (g, 0)), first, second, table, table],
        out_specs=pl.BlockSpec(shape, lambda g: (0, g, 0, 0)),
        scratch_shapes=[pltpu.VMEM((8 * TILES, LANES), jnp.float32), pltpu.VMEM((LANES, LANES), jnp.float32)],
        compiler_params=pltpu.CompilerParams(vmem_limit_bytes=12 * 2**20),
        cost_estimate=pl.CostEstimate(flops=2**25, bytes_accessed=2**23, transcendentals=0),
        name="finish",
    )(occ, own_occ, got, *ladders, va, vb)


def after_kernel(x_ref, *refs):
    refs[-1][...] = x_ref[...]


def after(x, *first):
    vmem = pl.BlockSpec(memory_space=pltpu.VMEM)
    return pl.pallas_call(
        after_kernel,
        out_shape=jax.ShapeDtypeStruct(x.shape, x.dtype),
        in_specs=[vmem] * (1 + len(first)),
        out_specs=vmem,
        compiler_params=pltpu.CompilerParams(vmem_limit_bytes=12 * 2**20),
        name="after",
    )(x, *first)


CHUNKS = (16, 16)


def per_device(amplitudes, integrals, cd_tiles, tile_counts, eps_occ, eps_virt):
    rows, partners, tiles, depth = amplitudes.shape
    slots = integrals.shape[1]
    me = lax.axis_index("virt")
    swap = [(v, v ^ 1) for v in range(VIRT)]
    relay = [(v, v + 2) for v in range(0, VIRT - 2, 2)] + [(v, v - 2) for v in range(3, VIRT, 2)]
    own, begin = [], 0
    for devices in CHUNKS:
        part = amplitudes[:, begin * rows : (begin + devices) * rows]
        own.append(jnp.transpose(part, (2, 0, 1, 3)).reshape(tiles, rows * rows * devices, depth))
        begin += devices
    live = lax.broadcasted_iota(jnp.int32, cd_tiles.shape, 1) < tile_counts[:, None]
    block = cd_tiles // tiles - me
    over_block = jnp.where(me % 2 == 0, 1, -1)
    place = jnp.where(block == 0, 0, jnp.where(block == over_block, 1, 2))
    index = jnp.where(live, place * tiles + cd_tiles % tiles, 3 * tiles).astype(jnp.int32)

    weights = integrals.reshape(tiles, slots * depth, LANES)

    def swapped(x):
        return lax.ppermute(x, "virt", swap)

    def passed_on(x):
        return lax.ppermute(x, "virt", relay)

    half = tiles // 2
    over_a = [swapped(own[0][:half]), swapped(own[0][half:])]
    over_b = [swapped(after(own[1][:half], over_a[0])), swapped(after(own[1][half:], over_a[0]))]
    beyond_a = [passed_on(x) for x in over_a]
    beyond_b = [passed_on(x) for x in over_b]
    beyond_a = [after(beyond_a[0], beyond_a[1]), beyond_a[1]]
    ladders = [
        ladder_rows(index, [own[0], *over_a, *beyond_a], weights),
        ladder_rows(index, [own[1], *over_b, *beyond_b], weights),
    ]
    sent = pack(ladders[1], pack(ladders[0])).astype(jnp.float16).reshape(-1, MSG // 2, 2, LANES)
    got = lax.all_to_all(sent, ("pair", "virt"), split_axis=0, concat_axis=0, tiled=True)
    own_occ = lax.dynamic_slice_in_dim(eps_occ, lax.axis_index("pair") * rows, rows)
    own_virt = lax.dynamic_slice_in_dim(eps_virt, me * tiles, tiles)
    va = jnp.broadcast_to(own_virt[:, None], (tiles, LANES))
    vb = jnp.broadcast_to(eps_virt[None, :], (tiles, LANES))
    ladders = [x.reshape(rows, -1, tiles, LANES) for x in ladders]
    return finish(eps_occ, own_occ, got.reshape(-1, LANES).astype(jnp.float32), ladders, va, vb)


def solution(mesh):
    in_specs = (
        P("pair", None, "virt", None),
        P("virt", None, None, None),
        P("virt", None),
        P("virt"),
        P(),
        P(),
    )
    out_specs = P("pair", None, "virt", None)
    return jax.shard_map(
        per_device, mesh=mesh, in_specs=in_specs, out_specs=out_specs, check_vma=False
    )
```

```python
import functools

import jax
import jax.numpy as jnp
from jax import lax
from jax.experimental import pallas as pl
from jax.experimental.pallas import tpu as pltpu
from jax.sharding import PartitionSpec as P

ROWS = 3
TILES = 16
VIRT = 8
LANES = 128
VALUES = ROWS * ROWS * TILES * TILES // LANES
MSG = VALUES + 2


def exchange_groups(parts):
    parts = list(parts)
    group = lax.broadcasted_iota(jnp.int32, parts[0].shape, 1) // TILES
    for step in (1, 2, 4):
        upper = (group & step) != 0
        for p in range(8):
            if p & step:
                continue
            low, high = parts[p], parts[p + step]
            parts[p] = jnp.where(upper, pltpu.roll(high, TILES * step, 1), low)
            parts[p + step] = jnp.where(upper, high, pltpu.roll(low, LANES - TILES * step, 1))
    return parts


def packer(ladder_ref, rest):
    devices = ladder_ref.shape[0] // (VIRT * VALUES)
    tile = ROWS * TILES
    row = devices * tile

    def widest(step, so_far):
        return jnp.maximum(so_far, jnp.abs(ladder_ref[pl.ds(pl.multiple_of(step * tile, TILES), tile), :]))

    largest = lax.fori_loop(0, ROWS * devices, widest, jnp.zeros((tile, LANES), jnp.float32), unroll=4)
    largest = jnp.maximum(jnp.max(jnp.max(largest, axis=0, keepdims=True), axis=1, keepdims=True), 1e-30)
    power = 14.0 - jnp.ceil(jnp.log2(jnp.broadcast_to(largest, (2, LANES))))
    scale = jnp.exp2(power)[:1]

    for octet in range(devices // 8):
        for half in range(2):
            first = octet * 8 * tile + (ROWS - 1) * (row + TILES) + half * 8
            parts = [ladder_ref[pl.ds(first + n, 8, stride=tile), :] for n in range(8)]
            for v, part in enumerate(exchange_groups(parts)):
                rest[pl.ds(octet * 8 * TILES + 2 * v + half, 8, stride=TILES), :] = part

    def rows(device):
        first = device * tile
        parts = [ladder_ref[pl.ds(first + (k // ROWS) * row + (k % ROWS) * TILES, TILES), :] * scale for k in range(8)]
        last = rest[pl.ds(device * TILES, TILES), :] * scale
        pieces = []
        for v, part in enumerate(exchange_groups(parts)):
            pieces += [part, last[2 * v : 2 * v + 2], power]
        return jnp.concatenate(pieces, axis=0)

    return devices, rows


WAITS = (1, 1, 2, 4, 4, 4)
AHEAD = 4


def ladder_kernel(packs, index_ref, *refs):
    columns_refs, refs = refs[: len(refs) - 6 - 3 * packs], refs[len(refs) - 6 - 3 * packs :]
    weight_ref, refs = refs[0], refs[1:]
    if packs:
        earlier_ref, out_ref, message_ref, held, weights, landed, arrived, rest = refs
    else:
        out_ref, held, weights, landed, arrived = refs
    slots = weight_ref.shape[1] // LANES

    def fetch(a):
        return pltpu.make_async_copy(weight_ref.at[a], weights.at[a], arrived.at[a])

    columns, begin = [], 0
    for n, ref in enumerate(columns_refs):
        place = held.at[pl.ds(begin, ref.shape[0])]
        columns.append(pltpu.make_async_copy(ref, place, landed.at[n]))
        begin += ref.shape[0]
    for copy in columns:
        copy.start()
    for a in range(AHEAD):
        fetch(a).start()
    held[3 * TILES] = jnp.zeros_like(held[3 * TILES])
    devices, rows = packer(earlier_ref, rest) if packs else (0, None)
    for copy in columns:
        copy.wait()
    first = 0
    for count in WAITS:
        for a in range(first, first + count):
            fetch(a).wait()
            if a + AHEAD < TILES:
                fetch(a + AHEAD).start()
        for a in range(first, first + count):
            row = None
            for s in range(0, slots, 4):
                four = jnp.concatenate([held[index_ref[a, s + t]] for t in range(4)], axis=1)
                part = weights[a, s * LANES : (s + 4) * LANES]
                term = jnp.dot(four, part, preferred_element_type=jnp.float32)
                row = term if row is None else row + term
            out_ref[pl.ds(a, row.shape[0], stride=TILES), :] = row
            for device in range(a * devices // TILES, (a + 1) * devices // TILES):
                message_ref[device * VIRT * MSG : (device + 1) * VIRT * MSG, :] = rows(device)
        first += count


def ladder_rows(index, columns, weights, earlier=None):
    pairs, depth = columns[0].shape[1:]
    tiles, k = weights.shape[:2]
    anywhere, vmem = pl.BlockSpec(memory_space=pl.ANY), pl.BlockSpec(memory_space=pltpu.VMEM)
    packs = earlier is not None
    out_shape = [jax.ShapeDtypeStruct((pairs * tiles, LANES), jnp.float32)]
    scratch = [
        pltpu.VMEM((3 * tiles + 1, pairs, depth), jnp.bfloat16),
        pltpu.VMEM(weights.shape, jnp.bfloat16),
        pltpu.SemaphoreType.DMA((len(columns),)),
        pltpu.SemaphoreType.DMA((tiles,)),
    ]
    if packs:
        out_shape.append(jax.ShapeDtypeStruct((earlier.shape[0] // VALUES * MSG, LANES), jnp.float32))
        scratch.append(pltpu.VMEM((earlier.shape[0] // (ROWS * ROWS), LANES), jnp.float32))
    return pl.pallas_call(
        functools.partial(ladder_kernel, int(packs)),
        out_shape=out_shape,
        in_specs=[pl.BlockSpec(memory_space=pltpu.SMEM)] + [anywhere] * (len(columns) + 1) + [vmem] * packs,
        out_specs=[vmem] * len(out_shape),
        scratch_shapes=scratch,
        compiler_params=pltpu.CompilerParams(vmem_limit_bytes=48 * 2**20),
        cost_estimate=pl.CostEstimate(
            flops=2 * pairs * k * LANES * tiles, bytes_accessed=2 * tiles * k * LANES, transcendentals=0
        ),
        name="ladder_rows",
    )(index, *columns, weights, *([earlier] if packs else []))


def pack_kernel(ladder_ref, earlier_ref, out_ref, rest):
    begin = earlier_ref.shape[0]
    out_ref[:begin, :] = earlier_ref[...]
    devices, rows = packer(ladder_ref, rest)
    for device in range(devices):
        out_ref[begin + device * VIRT * MSG : begin + (device + 1) * VIRT * MSG, :] = rows(device)


def pack(ladder, earlier):
    rows = ladder.shape[0]
    vmem = pl.BlockSpec(memory_space=pltpu.VMEM)
    return pl.pallas_call(
        pack_kernel,
        out_shape=jax.ShapeDtypeStruct((earlier.shape[0] + rows // VALUES * MSG, LANES), jnp.float32),
        in_specs=[vmem, vmem],
        out_specs=vmem,
        scratch_shapes=[pltpu.VMEM((rows // (ROWS * ROWS), LANES), jnp.float32)],
        compiler_params=pltpu.CompilerParams(vmem_limit_bytes=12 * 2**20),
        cost_estimate=pl.CostEstimate(flops=rows * LANES * 32, bytes_accessed=rows * LANES * 8, transcendentals=0),
        name="pack",
    )(ladder, earlier)


def finish_kernel(occ_ref, own_occ_ref, got_ref, first_ref, second_ref, va_ref, vb_ref, out_ref, rest, turned):
    step = pl.program_id(0)
    half = pl.num_programs(0) // 2

    def work(ladder_ref):
        def store(i, j, partner):
            bottom = (own_occ_ref[i] + occ_ref[step * 8 * ROWS + j]) - va_ref[...] - vb_ref[...]
            own = ladder_ref[i, lax.rem(step, half) * 8 * ROWS + j]
            out_ref[i, j] = ((own + partner) * (1.0 / bottom)).astype(out_ref.dtype)

        for device in range(8):
            first = pl.multiple_of((step * 8 + device) * VIRT * MSG, TILES)
            block = got_ref[pl.ds(first, VIRT * MSG), :]
            cut = [block[v * MSG : (v + 1) * MSG] for v in range(VIRT)]
            cut = [c[:VALUES] * jnp.exp2(-c[VALUES : VALUES + 1]) for c in cut]
            main = jnp.concatenate([c[:TILES] for c in cut], axis=0).T
            rest[device * TILES : (device + 1) * TILES, :] = jnp.concatenate([c[TILES:] for c in cut], axis=0)
            for k in range(8):
                store(k % ROWS, device * ROWS + k // ROWS, main[k * TILES : (k + 1) * TILES])
        for side in range(2):
            parts = [rest[pl.ds(2 * v + side, 8, stride=TILES), :] for v in range(VIRT)]
            for n, part in enumerate(exchange_groups(parts)):
                turned[pl.ds(side * 8 + n, 8, stride=TILES), :] = part
        columns = turned[...].T
        parts = [columns[v * TILES : (v + 1) * TILES] for v in range(VIRT)]
        for n, part in enumerate(exchange_groups(parts)):
            store(ROWS - 1, n * ROWS + ROWS - 1, part)

    @pl.when(step < half)
    def _():
        work(first_ref)

    @pl.when(step >= half)
    def _():
        work(second_ref)


def finish(occ, own_occ, got, ladders, va, vb):
    rows, partners = own_occ.shape[0], occ.shape[0]
    steps = partners // (8 * rows)
    smem = pl.BlockSpec(memory_space=pltpu.SMEM)
    shape = (rows, 8 * rows, TILES, LANES)
    vmem = pl.BlockSpec(memory_space=pltpu.VMEM)
    return pl.pallas_call(
        finish_kernel,
        out_shape=jax.ShapeDtypeStruct((rows, partners, TILES, LANES), jnp.bfloat16),
        grid=(steps,),
        in_specs=[smem, smem, vmem, vmem, vmem, vmem, vmem],
        out_specs=pl.BlockSpec(shape, lambda g: (0, g, 0, 0)),
        scratch_shapes=[pltpu.VMEM((8 * TILES, LANES), jnp.float32), pltpu.VMEM((LANES, LANES), jnp.float32)],
        compiler_params=pltpu.CompilerParams(vmem_limit_bytes=12 * 2**20),
        cost_estimate=pl.CostEstimate(flops=2**25, bytes_accessed=2**23, transcendentals=0),
        name="finish",
    )(occ, own_occ, got, *ladders, va, vb)


def after_kernel(x_ref, *refs):
    refs[-1][...] = x_ref[...]


def after(x, *first):
    vmem = pl.BlockSpec(memory_space=pltpu.VMEM)
    return pl.pallas_call(
        after_kernel,
        out_shape=jax.ShapeDtypeStruct(x.shape, x.dtype),
        in_specs=[vmem] * (1 + len(first)),
        out_specs=vmem,
        compiler_params=pltpu.CompilerParams(vmem_limit_bytes=12 * 2**20),
        name="after",
    )(x, *first)


CHUNKS = (16, 16)


def per_device(amplitudes, integrals, cd_tiles, tile_counts, eps_occ, eps_virt):
    rows, partners, tiles, depth = amplitudes.shape
    slots = integrals.shape[1]
    me = lax.axis_index("virt")
    swap = [(v, v ^ 1) for v in range(VIRT)]
    relay = [(v, v + 2) for v in range(0, VIRT - 2, 2)] + [(v, v - 2) for v in range(3, VIRT, 2)]
    own, begin = [], 0
    for devices in CHUNKS:
        part = amplitudes[:, begin * rows : (begin + devices) * rows]
        own.append(jnp.transpose(part, (2, 0, 1, 3)).reshape(tiles, rows * rows * devices, depth))
        begin += devices
    live = lax.broadcasted_iota(jnp.int32, cd_tiles.shape, 1) < tile_counts[:, None]
    block = cd_tiles // tiles - me
    over_block = jnp.where(me % 2 == 0, 1, -1)
    place = jnp.where(block == 0, 0, jnp.where(block == over_block, 1, 2))
    index = jnp.where(live, place * tiles + cd_tiles % tiles, 3 * tiles).astype(jnp.int32)

    weights = integrals.reshape(tiles, slots * depth, LANES)

    def swapped(x):
        return lax.ppermute(x, "virt", swap)

    def passed_on(x):
        return lax.ppermute(x, "virt", relay)

    half = tiles // 2
    over_a = [swapped(own[0][:half]), swapped(own[0][half:])]
    over_b = [swapped(after(own[1][:half], over_a[0])), swapped(after(own[1][half:], over_a[0]))]
    beyond_a = [passed_on(x) for x in over_a]
    beyond_b = [passed_on(x) for x in over_b]
    beyond_a = [after(beyond_a[0], beyond_a[1]), beyond_a[1]]
    [ladder_a] = ladder_rows(index, [own[0], *over_a, *beyond_a], weights)
    ladder_b, messages = ladder_rows(index, [own[1], *over_b, *beyond_b], weights, ladder_a)
    ladders = [ladder_a, ladder_b]
    sent = pack(ladder_b, messages).astype(jnp.float16).reshape(-1, MSG // 2, 2, LANES)
    got = lax.all_to_all(sent, ("pair", "virt"), split_axis=0, concat_axis=0, tiled=True)
    own_occ = lax.dynamic_slice_in_dim(eps_occ, lax.axis_index("pair") * rows, rows)
    own_virt = lax.dynamic_slice_in_dim(eps_virt, me * tiles, tiles)
    va = jnp.broadcast_to(own_virt[:, None], (tiles, LANES))
    vb = jnp.broadcast_to(eps_virt[None, :], (tiles, LANES))
    ladders = [x.reshape(rows, -1, tiles, LANES) for x in ladders]
    return finish(eps_occ, own_occ, got.reshape(-1, LANES).astype(jnp.float32), ladders, va, vb)


def solution(mesh):
    in_specs = (
        P("pair", None, "virt", None),
        P("virt", None, None, None),
        P("virt", None),
        P("virt"),
        P(),
        P(),
    )
    out_specs = P("pair", None, "virt", None)
    return jax.shard_map(
        per_device, mesh=mesh, in_specs=in_specs, out_specs=out_specs, check_vma=False
    )
```

```python
import functools

import jax
import jax.numpy as jnp
from jax import lax
from jax.experimental import pallas as pl
from jax.experimental.pallas import tpu as pltpu
from jax.sharding import PartitionSpec as P

ROWS = 3
TILES = 16
VIRT = 8
LANES = 128
VALUES = ROWS * ROWS * TILES * TILES // LANES
MSG = VALUES + 2


def exchange_groups(parts):
    parts = list(parts)
    group = lax.broadcasted_iota(jnp.int32, parts[0].shape, 1) // TILES
    for step in (1, 2, 4):
        upper = (group & step) != 0
        for p in range(8):
            if p & step:
                continue
            low, high = parts[p], parts[p + step]
            parts[p] = jnp.where(upper, pltpu.roll(high, TILES * step, 1), low)
            parts[p + step] = jnp.where(upper, high, pltpu.roll(low, LANES - TILES * step, 1))
    return parts


def packer(ladder_ref, rest):
    devices = ladder_ref.shape[0] // (VIRT * VALUES)
    tile = ROWS * TILES
    row = devices * tile

    def widest(step, so_far):
        return jnp.maximum(so_far, jnp.abs(ladder_ref[pl.ds(pl.multiple_of(step * tile, TILES), tile), :]))

    largest = lax.fori_loop(0, ROWS * devices, widest, jnp.zeros((tile, LANES), jnp.float32), unroll=4)
    largest = jnp.maximum(jnp.max(jnp.max(largest, axis=0, keepdims=True), axis=1, keepdims=True), 1e-30)
    power = 14.0 - jnp.ceil(jnp.log2(jnp.broadcast_to(largest, (2, LANES))))
    scale = jnp.exp2(power)[:1]

    for octet in range(devices // 8):
        for half in range(2):
            first = octet * 8 * tile + (ROWS - 1) * (row + TILES) + half * 8
            parts = [ladder_ref[pl.ds(first + n, 8, stride=tile), :] for n in range(8)]
            for v, part in enumerate(exchange_groups(parts)):
                rest[pl.ds(octet * 8 * TILES + 2 * v + half, 8, stride=TILES), :] = part

    def rows(device):
        first = device * tile
        parts = [ladder_ref[pl.ds(first + (k // ROWS) * row + (k % ROWS) * TILES, TILES), :] * scale for k in range(8)]
        last = rest[pl.ds(device * TILES, TILES), :] * scale
        pieces = []
        for v, part in enumerate(exchange_groups(parts)):
            pieces += [part, last[2 * v : 2 * v + 2], power]
        return jnp.concatenate(pieces, axis=0)

    return devices, rows


WAITS = (2, 2, 4, 4, 4)
AHEAD = 8


def ladder_kernel(packs, index_ref, *refs):
    columns_refs, refs = refs[: len(refs) - 6 - 3 * packs], refs[len(refs) - 6 - 3 * packs :]
    weight_ref, refs = refs[0], refs[1:]
    if packs:
        earlier_ref, out_ref, message_ref, held, weights, landed, arrived, rest = refs
    else:
        out_ref, held, weights, landed, arrived = refs
    slots = weight_ref.shape[1] // LANES

    def fetch(a):
        return pltpu.make_async_copy(weight_ref.at[a], weights.at[a], arrived.at[a])

    columns, begin = [], 0
    for n, ref in enumerate(columns_refs):
        place = held.at[pl.ds(begin, ref.shape[0])]
        columns.append(pltpu.make_async_copy(ref, place, landed.at[n]))
        begin += ref.shape[0]
    for copy in columns:
        copy.start()
    for a in range(AHEAD):
        fetch(a).start()
    held[3 * TILES] = jnp.zeros_like(held[3 * TILES])
    devices, rows = packer(earlier_ref, rest) if packs else (0, None)
    for copy in columns:
        copy.wait()
    first = 0
    for count in WAITS:
        for a in range(first, first + count):
            fetch(a).wait()
            if a + AHEAD < TILES:
                fetch(a + AHEAD).start()
        for a in range(first, first + count):
            row = None
            for s in range(0, slots, 4):
                four = jnp.concatenate([held[index_ref[a, s + t]] for t in range(4)], axis=1)
                part = weights[a, s * LANES : (s + 4) * LANES]
                term = jnp.dot(four, part, preferred_element_type=jnp.float32)
                row = term if row is None else row + term
            out_ref[pl.ds(a, row.shape[0], stride=TILES), :] = row
            for device in range(a * devices // TILES, (a + 1) * devices // TILES):
                message_ref[device * VIRT * MSG : (device + 1) * VIRT * MSG, :] = rows(device)
        first += count


def ladder_rows(index, columns, weights, earlier=None):
    pairs, depth = columns[0].shape[1:]
    tiles, k = weights.shape[:2]
    anywhere, vmem = pl.BlockSpec(memory_space=pl.ANY), pl.BlockSpec(memory_space=pltpu.VMEM)
    packs = earlier is not None
    out_shape = [jax.ShapeDtypeStruct((pairs * tiles, LANES), jnp.float32)]
    scratch = [
        pltpu.VMEM((3 * tiles + 1, pairs, depth), jnp.bfloat16),
        pltpu.VMEM(weights.shape, jnp.bfloat16),
        pltpu.SemaphoreType.DMA((len(columns),)),
        pltpu.SemaphoreType.DMA((tiles,)),
    ]
    if packs:
        out_shape.append(jax.ShapeDtypeStruct((earlier.shape[0] // VALUES * MSG, LANES), jnp.float32))
        scratch.append(pltpu.VMEM((earlier.shape[0] // (ROWS * ROWS), LANES), jnp.float32))
    return pl.pallas_call(
        functools.partial(ladder_kernel, int(packs)),
        out_shape=out_shape,
        in_specs=[pl.BlockSpec(memory_space=pltpu.SMEM)] + [anywhere] * (len(columns) + 1) + [vmem] * packs,
        out_specs=[vmem] * len(out_shape),
        scratch_shapes=scratch,
        compiler_params=pltpu.CompilerParams(vmem_limit_bytes=48 * 2**20),
        cost_estimate=pl.CostEstimate(
            flops=2 * pairs * k * LANES * tiles, bytes_accessed=2 * tiles * k * LANES, transcendentals=0
        ),
        name="ladder_rows",
    )(index, *columns, weights, *([earlier] if packs else []))


def pack_kernel(ladder_ref, earlier_ref, out_ref, rest):
    begin = earlier_ref.shape[0]
    out_ref[:begin, :] = earlier_ref[...]
    devices, rows = packer(ladder_ref, rest)
    for device in range(devices):
        out_ref[begin + device * VIRT * MSG : begin + (device + 1) * VIRT * MSG, :] = rows(device)


def pack(ladder, earlier):
    rows = ladder.shape[0]
    vmem = pl.BlockSpec(memory_space=pltpu.VMEM)
    return pl.pallas_call(
        pack_kernel,
        out_shape=jax.ShapeDtypeStruct((earlier.shape[0] + rows // VALUES * MSG, LANES), jnp.float32),
        in_specs=[vmem, vmem],
        out_specs=vmem,
        scratch_shapes=[pltpu.VMEM((rows // (ROWS * ROWS), LANES), jnp.float32)],
        compiler_params=pltpu.CompilerParams(vmem_limit_bytes=12 * 2**20),
        cost_estimate=pl.CostEstimate(flops=rows * LANES * 32, bytes_accessed=rows * LANES * 8, transcendentals=0),
        name="pack",
    )(ladder, earlier)


def finish_kernel(occ_ref, own_occ_ref, got_ref, first_ref, second_ref, va_ref, vb_ref, out_ref, rest, turned):
    step = pl.program_id(0)
    half = pl.num_programs(0) // 2

    def work(ladder_ref):
        def store(i, j, partner):
            bottom = (own_occ_ref[i] + occ_ref[step * 8 * ROWS + j]) - va_ref[...] - vb_ref[...]
            own = ladder_ref[i, lax.rem(step, half) * 8 * ROWS + j]
            out_ref[i, j] = ((own + partner) * (1.0 / bottom)).astype(out_ref.dtype)

        for device in range(8):
            first = pl.multiple_of((step * 8 + device) * VIRT * MSG, TILES)
            block = got_ref[pl.ds(first, VIRT * MSG), :]
            cut = [block[v * MSG : (v + 1) * MSG] for v in range(VIRT)]
            cut = [c[:VALUES] * jnp.exp2(-c[VALUES : VALUES + 1]) for c in cut]
            main = jnp.concatenate([c[:TILES] for c in cut], axis=0).T
            rest[device * TILES : (device + 1) * TILES, :] = jnp.concatenate([c[TILES:] for c in cut], axis=0)
            for k in range(8):
                store(k % ROWS, device * ROWS + k // ROWS, main[k * TILES : (k + 1) * TILES])
        for side in range(2):
            parts = [rest[pl.ds(2 * v + side, 8, stride=TILES), :] for v in range(VIRT)]
            for n, part in enumerate(exchange_groups(parts)):
                turned[pl.ds(side * 8 + n, 8, stride=TILES), :] = part
        columns = turned[...].T
        parts = [columns[v * TILES : (v + 1) * TILES] for v in range(VIRT)]
        for n, part in enumerate(exchange_groups(parts)):
            store(ROWS - 1, n * ROWS + ROWS - 1, part)

    @pl.when(step < half)
    def _():
        work(first_ref)

    @pl.when(step >= half)
    def _():
        work(second_ref)


def finish(occ, own_occ, got, ladders, va, vb):
    rows, partners = own_occ.shape[0], occ.shape[0]
    steps = partners // (8 * rows)
    smem = pl.BlockSpec(memory_space=pltpu.SMEM)
    shape = (rows, 8 * rows, TILES, LANES)
    vmem = pl.BlockSpec(memory_space=pltpu.VMEM)
    return pl.pallas_call(
        finish_kernel,
        out_shape=jax.ShapeDtypeStruct((rows, partners, TILES, LANES), jnp.bfloat16),
        grid=(steps,),
        in_specs=[smem, smem, vmem, vmem, vmem, vmem, vmem],
        out_specs=pl.BlockSpec(shape, lambda g: (0, g, 0, 0)),
        scratch_shapes=[pltpu.VMEM((8 * TILES, LANES), jnp.float32), pltpu.VMEM((LANES, LANES), jnp.float32)],
        compiler_params=pltpu.CompilerParams(vmem_limit_bytes=12 * 2**20),
        cost_estimate=pl.CostEstimate(flops=2**25, bytes_accessed=2**23, transcendentals=0),
        name="finish",
    )(occ, own_occ, got, *ladders, va, vb)


def after_kernel(x_ref, *refs):
    refs[-1][...] = x_ref[...]


def after(x, *first):
    vmem = pl.BlockSpec(memory_space=pltpu.VMEM)
    return pl.pallas_call(
        after_kernel,
        out_shape=jax.ShapeDtypeStruct(x.shape, x.dtype),
        in_specs=[vmem] * (1 + len(first)),
        out_specs=vmem,
        compiler_params=pltpu.CompilerParams(vmem_limit_bytes=12 * 2**20),
        name="after",
    )(x, *first)


CHUNKS = (16, 16)


def per_device(amplitudes, integrals, cd_tiles, tile_counts, eps_occ, eps_virt):
    rows, partners, tiles, depth = amplitudes.shape
    slots = integrals.shape[1]
    me = lax.axis_index("virt")
    swap = [(v, v ^ 1) for v in range(VIRT)]
    relay = [(v, v + 2) for v in range(0, VIRT - 2, 2)] + [(v, v - 2) for v in range(3, VIRT, 2)]
    own, begin = [], 0
    for devices in CHUNKS:
        part = amplitudes[:, begin * rows : (begin + devices) * rows]
        own.append(jnp.transpose(part, (2, 0, 1, 3)).reshape(tiles, rows * rows * devices, depth))
        begin += devices
    live = lax.broadcasted_iota(jnp.int32, cd_tiles.shape, 1) < tile_counts[:, None]
    block = cd_tiles // tiles - me
    over_block = jnp.where(me % 2 == 0, 1, -1)
    place = jnp.where(block == 0, 0, jnp.where(block == over_block, 1, 2))
    index = jnp.where(live, place * tiles + cd_tiles % tiles, 3 * tiles).astype(jnp.int32)

    weights = integrals.reshape(tiles, slots * depth, LANES)

    def swapped(x):
        return lax.ppermute(x, "virt", swap)

    def passed_on(x):
        return lax.ppermute(x, "virt", relay)

    half = tiles // 2
    over_a = [swapped(own[0][:half]), swapped(own[0][half:])]
    over_b = [swapped(after(own[1][:half], over_a[0])), swapped(after(own[1][half:], over_a[0]))]
    beyond_a = [passed_on(x) for x in over_a]
    beyond_b = [passed_on(x) for x in over_b]
    beyond_a = [after(beyond_a[0], beyond_a[1]), beyond_a[1]]
    [ladder_a] = ladder_rows(index, [own[0], *over_a, *beyond_a], weights)
    ladder_b, messages = ladder_rows(index, [own[1], *over_b, *beyond_b], weights, ladder_a)
    ladders = [ladder_a, ladder_b]
    sent = pack(ladder_b, messages).astype(jnp.float16).reshape(-1, MSG // 2, 2, LANES)
    got = lax.all_to_all(sent, ("pair", "virt"), split_axis=0, concat_axis=0, tiled=True)
    own_occ = lax.dynamic_slice_in_dim(eps_occ, lax.axis_index("pair") * rows, rows)
    own_virt = lax.dynamic_slice_in_dim(eps_virt, me * tiles, tiles)
    va = jnp.broadcast_to(own_virt[:, None], (tiles, LANES))
    vb = jnp.broadcast_to(eps_virt[None, :], (tiles, LANES))
    ladders = [x.reshape(rows, -1, tiles, LANES) for x in ladders]
    return finish(eps_occ, own_occ, got.reshape(-1, LANES).astype(jnp.float32), ladders, va, vb)


def solution(mesh):
    in_specs = (
        P("pair", None, "virt", None),
        P("virt", None, None, None),
        P("virt", None),
        P("virt"),
        P(),
        P(),
    )
    out_specs = P("pair", None, "virt", None)
    return jax.shard_map(
        per_device, mesh=mesh, in_specs=in_specs, out_specs=out_specs, check_vma=False
    )
```

```python
import functools

import jax
import jax.numpy as jnp
from jax import lax
from jax.experimental import pallas as pl
from jax.experimental.pallas import tpu as pltpu
from jax.sharding import PartitionSpec as P

ROWS = 3
TILES = 16
VIRT = 8
LANES = 128
VALUES = ROWS * ROWS * TILES * TILES // LANES
MSG = VALUES + 2


def exchange_groups(parts):
    parts = list(parts)
    group = lax.broadcasted_iota(jnp.int32, parts[0].shape, 1) // TILES
    for step in (1, 2, 4):
        upper = (group & step) != 0
        for p in range(8):
            if p & step:
                continue
            low, high = parts[p], parts[p + step]
            parts[p] = jnp.where(upper, pltpu.roll(high, TILES * step, 1), low)
            parts[p + step] = jnp.where(upper, high, pltpu.roll(low, LANES - TILES * step, 1))
    return parts


def packer(ladder_ref, rest):
    devices = ladder_ref.shape[0] // (VIRT * VALUES)
    tile = ROWS * TILES
    row = devices * tile

    def widest(step, so_far):
        return jnp.maximum(so_far, jnp.abs(ladder_ref[pl.ds(pl.multiple_of(step * tile, TILES), tile), :]))

    largest = lax.fori_loop(0, ROWS * devices, widest, jnp.zeros((tile, LANES), jnp.float32), unroll=4)
    largest = jnp.maximum(jnp.max(jnp.max(largest, axis=0, keepdims=True), axis=1, keepdims=True), 1e-30)
    power = 14.0 - jnp.ceil(jnp.log2(jnp.broadcast_to(largest, (2, LANES))))
    scale = jnp.exp2(power)[:1]

    for octet in range(devices // 8):
        for half in range(2):
            first = octet * 8 * tile + (ROWS - 1) * (row + TILES) + half * 8
            parts = [ladder_ref[pl.ds(first + n, 8, stride=tile), :] for n in range(8)]
            for v, part in enumerate(exchange_groups(parts)):
                rest[pl.ds(octet * 8 * TILES + 2 * v + half, 8, stride=TILES), :] = part

    def rows(device):
        first = device * tile
        parts = [ladder_ref[pl.ds(first + (k // ROWS) * row + (k % ROWS) * TILES, TILES), :] * scale for k in range(8)]
        last = rest[pl.ds(device * TILES, TILES), :] * scale
        pieces = []
        for v, part in enumerate(exchange_groups(parts)):
            pieces += [part, last[2 * v : 2 * v + 2], power]
        return jnp.concatenate(pieces, axis=0)

    return devices, rows


WAITS = (2, 2, 4, 4, 4)
AHEAD = 8


def ladder_kernel(packs, index_ref, *refs):
    columns_refs, refs = refs[: len(refs) - 6 - 3 * packs], refs[len(refs) - 6 - 3 * packs :]
    weight_ref, refs = refs[0], refs[1:]
    if packs:
        earlier_ref, out_ref, message_ref, held, weights, landed, arrived, rest = refs
    else:
        out_ref, held, weights, landed, arrived = refs
    slots = weight_ref.shape[1] // LANES

    def fetch(a):
        return pltpu.make_async_copy(weight_ref.at[a], weights.at[a], arrived.at[a])

    columns, begin = [], 0
    for n, ref in enumerate(columns_refs):
        place = held.at[pl.ds(begin, ref.shape[0])]
        columns.append(pltpu.make_async_copy(ref, place, landed.at[n]))
        begin += ref.shape[0]
    for copy in columns:
        copy.start()
    for a in range(AHEAD):
        fetch(a).start()
    held[3 * TILES] = jnp.zeros_like(held[3 * TILES])
    devices, rows = packer(earlier_ref, rest) if packs else (0, None)
    for copy in columns:
        copy.wait()
    first = 0
    for count in WAITS:
        for a in range(first, first + count):
            fetch(a).wait()
            if a + AHEAD < TILES:
                fetch(a + AHEAD).start()
        for a in range(first, first + count):
            row = None
            for s in range(0, slots, 4):
                four = jnp.concatenate([held[index_ref[a, s + t]] for t in range(4)], axis=1)
                part = weights[a, s * LANES : (s + 4) * LANES]
                term = jnp.dot(four, part, preferred_element_type=jnp.float32)
                row = term if row is None else row + term
            out_ref[pl.ds(a, row.shape[0], stride=TILES), :] = row
            for device in range(a * devices // TILES, (a + 1) * devices // TILES):
                message_ref[device * VIRT * MSG : (device + 1) * VIRT * MSG, :] = rows(device)
        first += count


def ladder_rows(index, columns, weights, earlier=None):
    pairs, depth = columns[0].shape[1:]
    tiles, k = weights.shape[:2]
    anywhere, vmem = pl.BlockSpec(memory_space=pl.ANY), pl.BlockSpec(memory_space=pltpu.VMEM)
    packs = earlier is not None
    out_shape = [jax.ShapeDtypeStruct((pairs * tiles, LANES), jnp.float32)]
    scratch = [
        pltpu.VMEM((3 * tiles + 1, pairs, depth), jnp.bfloat16),
        pltpu.VMEM(weights.shape, jnp.bfloat16),
        pltpu.SemaphoreType.DMA((len(columns),)),
        pltpu.SemaphoreType.DMA((tiles,)),
    ]
    if packs:
        out_shape.append(jax.ShapeDtypeStruct((earlier.shape[0] // VALUES * MSG, LANES), jnp.float32))
        scratch.append(pltpu.VMEM((earlier.shape[0] // (ROWS * ROWS), LANES), jnp.float32))
    return pl.pallas_call(
        functools.partial(ladder_kernel, int(packs)),
        out_shape=out_shape,
        in_specs=[pl.BlockSpec(memory_space=pltpu.SMEM)] + [anywhere] * (len(columns) + 1) + [vmem] * packs,
        out_specs=[vmem] * len(out_shape),
        scratch_shapes=scratch,
        compiler_params=pltpu.CompilerParams(vmem_limit_bytes=48 * 2**20),
        cost_estimate=pl.CostEstimate(
            flops=2 * pairs * k * LANES * tiles, bytes_accessed=2 * tiles * k * LANES, transcendentals=0
        ),
        name="ladder_rows",
    )(index, *columns, weights, *([earlier] if packs else []))


def pack_kernel(ladder_ref, earlier_ref, out_ref, rest):
    begin = earlier_ref.shape[0]
    out_ref[:begin, :] = earlier_ref[...]
    devices, rows = packer(ladder_ref, rest)
    for device in range(devices):
        out_ref[begin + device * VIRT * MSG : begin + (device + 1) * VIRT * MSG, :] = rows(device)


def pack(ladder, earlier):
    rows = ladder.shape[0]
    vmem = pl.BlockSpec(memory_space=pltpu.VMEM)
    return pl.pallas_call(
        pack_kernel,
        out_shape=jax.ShapeDtypeStruct((earlier.shape[0] + rows // VALUES * MSG, LANES), jnp.float32),
        in_specs=[vmem, vmem],
        out_specs=vmem,
        scratch_shapes=[pltpu.VMEM((rows // (ROWS * ROWS), LANES), jnp.float32)],
        compiler_params=pltpu.CompilerParams(vmem_limit_bytes=12 * 2**20),
        cost_estimate=pl.CostEstimate(flops=rows * LANES * 32, bytes_accessed=rows * LANES * 8, transcendentals=0),
        name="pack",
    )(ladder, earlier)


def finish_kernel(occ_ref, own_occ_ref, got_ref, first_ref, second_ref, va_ref, vb_ref, out_ref, rest, turned):
    step = pl.program_id(0)
    split = first_ref.shape[1] // (8 * ROWS)

    def work(ladder_ref, since):
        def store(i, j, partner):
            bottom = (own_occ_ref[i] + occ_ref[step * 8 * ROWS + j]) - va_ref[...] - vb_ref[...]
            own = ladder_ref[i, (step - since) * 8 * ROWS + j]
            out_ref[i, j] = ((own + partner) * (1.0 / bottom)).astype(out_ref.dtype)

        for device in range(8):
            first = pl.multiple_of((step * 8 + device) * VIRT * MSG, TILES)
            block = got_ref[pl.ds(first, VIRT * MSG), :]
            cut = [block[v * MSG : (v + 1) * MSG] for v in range(VIRT)]
            cut = [c[:VALUES] * jnp.exp2(-c[VALUES : VALUES + 1]) for c in cut]
            main = jnp.concatenate([c[:TILES] for c in cut], axis=0).T
            rest[device * TILES : (device + 1) * TILES, :] = jnp.concatenate([c[TILES:] for c in cut], axis=0)
            for k in range(8):
                store(k % ROWS, device * ROWS + k // ROWS, main[k * TILES : (k + 1) * TILES])
        for side in range(2):
            parts = [rest[pl.ds(2 * v + side, 8, stride=TILES), :] for v in range(VIRT)]
            for n, part in enumerate(exchange_groups(parts)):
                turned[pl.ds(side * 8 + n, 8, stride=TILES), :] = part
        columns = turned[...].T
        parts = [columns[v * TILES : (v + 1) * TILES] for v in range(VIRT)]
        for n, part in enumerate(exchange_groups(parts)):
            store(ROWS - 1, n * ROWS + ROWS - 1, part)

    @pl.when(step < split)
    def _():
        work(first_ref, 0)

    @pl.when(step >= split)
    def _():
        work(second_ref, split)


def finish(occ, own_occ, got, ladders, va, vb):
    rows, partners = own_occ.shape[0], occ.shape[0]
    steps = partners // (8 * rows)
    smem = pl.BlockSpec(memory_space=pltpu.SMEM)
    shape = (rows, 8 * rows, TILES, LANES)
    vmem = pl.BlockSpec(memory_space=pltpu.VMEM)
    return pl.pallas_call(
        finish_kernel,
        out_shape=jax.ShapeDtypeStruct((rows, partners, TILES, LANES), jnp.bfloat16),
        grid=(steps,),
        in_specs=[smem, smem, vmem, vmem, vmem, vmem, vmem],
        out_specs=pl.BlockSpec(shape, lambda g: (0, g, 0, 0)),
        scratch_shapes=[pltpu.VMEM((8 * TILES, LANES), jnp.float32), pltpu.VMEM((LANES, LANES), jnp.float32)],
        compiler_params=pltpu.CompilerParams(vmem_limit_bytes=12 * 2**20),
        cost_estimate=pl.CostEstimate(flops=2**25, bytes_accessed=2**23, transcendentals=0),
        name="finish",
    )(occ, own_occ, got, *ladders, va, vb)


def after_kernel(x_ref, *refs):
    refs[-1][...] = x_ref[...]


def after(x, *first):
    vmem = pl.BlockSpec(memory_space=pltpu.VMEM)
    return pl.pallas_call(
        after_kernel,
        out_shape=jax.ShapeDtypeStruct(x.shape, x.dtype),
        in_specs=[vmem] * (1 + len(first)),
        out_specs=vmem,
        compiler_params=pltpu.CompilerParams(vmem_limit_bytes=12 * 2**20),
        name="after",
    )(x, *first)


CHUNKS = (24, 8)


def per_device(amplitudes, integrals, cd_tiles, tile_counts, eps_occ, eps_virt):
    rows, partners, tiles, depth = amplitudes.shape
    slots = integrals.shape[1]
    me = lax.axis_index("virt")
    swap = [(v, v ^ 1) for v in range(VIRT)]
    relay = [(v, v + 2) for v in range(0, VIRT - 2, 2)] + [(v, v - 2) for v in range(3, VIRT, 2)]
    own, begin = [], 0
    for devices in CHUNKS:
        part = amplitudes[:, begin * rows : (begin + devices) * rows]
        own.append(jnp.transpose(part, (2, 0, 1, 3)).reshape(tiles, rows * rows * devices, depth))
        begin += devices
    live = lax.broadcasted_iota(jnp.int32, cd_tiles.shape, 1) < tile_counts[:, None]
    block = cd_tiles // tiles - me
    over_block = jnp.where(me % 2 == 0, 1, -1)
    place = jnp.where(block == 0, 0, jnp.where(block == over_block, 1, 2))
    index = jnp.where(live, place * tiles + cd_tiles % tiles, 3 * tiles).astype(jnp.int32)

    weights = integrals.reshape(tiles, slots * depth, LANES)

    def swapped(x):
        return lax.ppermute(x, "virt", swap)

    def passed_on(x):
        return lax.ppermute(x, "virt", relay)

    half = tiles // 2
    over_a = [swapped(own[0][:half]), swapped(own[0][half:])]
    over_b = [swapped(after(own[1], over_a[0]))]
    beyond_a = [passed_on(x) for x in over_a]
    beyond_b = [passed_on(x) for x in over_b]
    beyond_a = [after(beyond_a[0], beyond_a[1]), beyond_a[1]]
    [ladder_a] = ladder_rows(index, [own[0], *over_a, *beyond_a], weights)
    ladder_b, messages = ladder_rows(index, [own[1], *over_b, *beyond_b], weights, ladder_a)
    ladders = [ladder_a, ladder_b]
    sent = pack(ladder_b, messages).astype(jnp.float16).reshape(-1, MSG // 2, 2, LANES)
    got = lax.all_to_all(sent, ("pair", "virt"), split_axis=0, concat_axis=0, tiled=True)
    own_occ = lax.dynamic_slice_in_dim(eps_occ, lax.axis_index("pair") * rows, rows)
    own_virt = lax.dynamic_slice_in_dim(eps_virt, me * tiles, tiles)
    va = jnp.broadcast_to(own_virt[:, None], (tiles, LANES))
    vb = jnp.broadcast_to(eps_virt[None, :], (tiles, LANES))
    ladders = [x.reshape(rows, -1, tiles, LANES) for x in ladders]
    return finish(eps_occ, own_occ, got.reshape(-1, LANES).astype(jnp.float32), ladders, va, vb)


def solution(mesh):
    in_specs = (
        P("pair", None, "virt", None),
        P("virt", None, None, None),
        P("virt", None),
        P("virt"),
        P(),
        P(),
    )
    out_specs = P("pair", None, "virt", None)
    return jax.shard_map(
        per_device, mesh=mesh, in_specs=in_specs, out_specs=out_specs, check_vma=False
    )
```
